32 devices in a mesh: seq: 8 (over z, y), dp: 4 (over x, core).
Axes of the slice: x: 2, y: 2, z: 4, core: 2. Of those that a mesh axis runs over, the one named last changes fastest.
Arguments:
- inputs: float32 [4, 4096, 128], P('dp', 'seq'), may hold values from -6 to 6
- gate_values: float32 [4, 4096, 128], P('dp', 'seq'), may hold values from -6 to 6
- out_grad: float32 [4, 4096, 128], P('dp', 'seq'), may hold values from -6 to 6
- filter_taps: float32 [4096, 128], P('seq'), may hold values from -0.09375 to 0.09375
- skip_gain: float32 [128], replicated, may hold values from -4 to 4
Outputs:
- input_grad: float32 [4, 4096, 128], P('dp', 'seq')
- gate_grad: float32 [4, 4096, 128], P('dp', 'seq')
- filter_grad: float32 [4096, 128], P('seq', 'dp')
The draws below stay inside these ranges and needn't reach their ends.
All inputs are finite; a program needn't handle non-finite values.
Results may differ from the reference program's by a relative error of at most 0.0001.
Values sent between devices are 32-bit elements; how exact they have to be, the bound alone decides.
A program may use at most 64 MiB of HBM per device.

```python
import math
import jax
import jax.numpy as jnp
from jax import lax

CH = 128
LENGTH = 4096
BATCH = 4


def block_levels(own_key, shape, shards, low, top_value):
    loudness = 1.0
    for dim, shards_of in shards:
        draws = jax.random.uniform(jax.random.fold_in(jax.random.fold_in(own_key, 6), dim), (shards_of,), jnp.float32, low / len(shards), top_value / len(shards))
        loudness = loudness * jnp.repeat(jnp.exp(draws), shape[dim] // shards_of).reshape((-1,) + (1,) * (len(shape) - 1 - dim))
    return loudness


def centred(stream_key, dims, width, bound, cuts=(), held_as=jnp.bfloat16):
    array = width * jax.random.normal(stream_key, dims, jnp.float32)
    if cuts:
        array = array * block_levels(stream_key, dims, cuts, -0.22, 0.18)
    return jnp.clip(array, -bound, bound).astype(held_as)


def setup_inputs(seed: int = 0) -> dict:
    key_list = jax.random.split(jax.random.key(seed), 6)
    inputs = centred(key_list[0], (BATCH, LENGTH, CH), 1.0, 6.0, ((0, 4), (1, 8)), jnp.float32)
    gate_values = centred(key_list[1], (BATCH, LENGTH, CH), 1.0, 6.0, ((0, 4), (1, 8)), jnp.float32)
    out_grad = centred(key_list[2], (BATCH, LENGTH, CH), 1.0, 6.0, ((0, 4), (1, 8)), jnp.float32)
    filter_taps = centred(key_list[3], (LENGTH, CH), LENGTH ** -0.5, 0.09375, ((0, 8),), jnp.float32)
    skip_gain = centred(key_list[4], (CH,), 1.0, 4.0, (), jnp.float32)
    return dict(inputs=inputs, gate_values=gate_values, out_grad=out_grad, filter_taps=filter_taps, skip_gain=skip_gain)


def reference(inputs, gate_values, out_grad, filter_taps, skip_gain):
    total = 2 * LENGTH
    filter_spec = jnp.fft.rfft(filter_taps, n=total, axis=0)

    def one_sequence(operands):
        seq_input, seq_gate, seq_grad = operands
        conv_grad = seq_grad * seq_gate
        input_spec = jnp.fft.rfft(seq_input, n=total, axis=0)
        grad_spec = jnp.fft.rfft(conv_grad, n=total, axis=0)
        conv_time = jnp.fft.irfft(filter_spec * input_spec, n=total, axis=0)[:LENGTH].astype(jnp.float32)
        gate_part = seq_grad * (conv_time + skip_gain[None, :] * seq_input)
        corr_time = jnp.fft.irfft(jnp.conj(filter_spec) * grad_spec, n=total, axis=0)[:LENGTH].astype(jnp.float32)
        input_part = corr_time + skip_gain[None, :] * conv_grad
        filter_part = jnp.fft.irfft(jnp.conj(input_spec) * grad_spec, n=total, axis=0)[:LENGTH].astype(jnp.float32)
        return (input_part, gate_part, filter_part)
    input_grad, gate_grad, filter_parts = lax.map(one_sequence, (inputs, gate_values, out_grad))
    filter_grad = lax.optimization_barrier(jnp.sum(filter_parts, axis=0)) / math.sqrt(BATCH * LENGTH)
    return (input_grad, gate_grad, filter_grad)
```

```python
import functools
import math

import jax
import jax.numpy as jnp
import ml_dtypes
import numpy as np
from jax import lax
from jax.experimental import pallas as pl
from jax.experimental.pallas import tpu as pltpu
from jax.sharding import PartitionSpec as P

first_radix = 32


def rotation(product, modulus, direction):
    fraction = (product % modulus).astype(jnp.float32) / modulus
    turned = 2.0 * math.pi * fraction
    return (jnp.cos(turned), direction * jnp.sin(turned))


def contract(formula, matrix, operand):
    return jnp.einsum(
        formula,
        matrix,
        operand,
        precision=lax.Precision.HIGHEST,
        preferred_element_type=jnp.float32,
    )


def complex_apply(formula, table_re, table_im, values_re, values_im):
    result_re = contract(formula, table_re, values_re) - contract(formula, table_im, values_im)
    result_im = contract(formula, table_re, values_im) + contract(formula, table_im, values_re)
    return (result_re, result_im)


def local_forward(values_re, values_im):
    pairs, rows, width = values_re.shape
    second = rows // first_radix
    values_re = values_re.reshape(pairs, first_radix, second, width)
    values_im = values_im.reshape(pairs, first_radix, second, width)
    outer = jnp.arange(first_radix, dtype=jnp.int32)
    inner = jnp.arange(second, dtype=jnp.int32)
    table_re, table_im = rotation(outer[:, None] * outer[None, :], first_radix, -1.0)
    section_re, section_im = complex_apply(
        "ca,mabx->mcbx", table_re, table_im, values_re, values_im
    )
    twist_re, twist_im = rotation(outer[:, None] * inner[None, :], rows, -1.0)
    twist_re = twist_re[None, :, :, None]
    twist_im = twist_im[None, :, :, None]
    turned_re = section_re * twist_re - section_im * twist_im
    turned_im = section_re * twist_im + section_im * twist_re
    table_re, table_im = rotation(inner[:, None] * inner[None, :], second, -1.0)
    return complex_apply("db,mcbx->mcdx", table_re, table_im, turned_re, turned_im)


def local_inverse(spec_re, spec_im):
    pairs, first, second, width = spec_re.shape
    rows = first * second
    outer = jnp.arange(first, dtype=jnp.int32)
    inner = jnp.arange(second, dtype=jnp.int32)
    table_re, table_im = rotation(inner[:, None] * inner[None, :], second, 1.0)
    section_re, section_im = complex_apply("bd,mcdx->mcbx", table_re, table_im, spec_re, spec_im)
    twist_re, twist_im = rotation(outer[:, None] * inner[None, :], rows, 1.0)
    twist_re = twist_re[None, :, :, None]
    twist_im = twist_im[None, :, :, None]
    turned_re = section_re * twist_re - section_im * twist_im
    turned_im = section_re * twist_im + section_im * twist_re
    table_re, table_im = rotation(outer[:, None] * outer[None, :], first, 1.0)
    result_re, result_im = complex_apply("ac,mcbx->mabx", table_re, table_im, turned_re, turned_im)
    return (result_re.reshape(pairs, rows, width), result_im.reshape(pairs, rows, width))


def frequency_labels():
    steps = lax.axis_size("seq")
    own = lax.axis_index("seq")
    local_labels = 2 * own + jnp.arange(2, dtype=jnp.int32)
    all_labels = jnp.arange(2 * steps, dtype=jnp.int32)
    return (local_labels, all_labels)


def forward_spectrum(signal):
    rows, width = signal.shape
    steps = lax.axis_size("seq")
    piece = rows // steps
    double = 2 * steps
    total = double * rows
    columns = lax.all_to_all(
        signal.reshape(1, rows, width), "seq", split_axis=1, concat_axis=0, tiled=True
    )
    block_index = jnp.arange(steps, dtype=jnp.int32)
    freq_index = jnp.arange(double, dtype=jnp.int32)
    table_re, table_im = rotation(freq_index[:, None] * block_index[None, :], double, -1.0)
    coarse_re = contract("kq,qrc->krc", table_re, columns)
    coarse_im = contract("kq,qrc->krc", table_im, columns)
    offsets = lax.axis_index("seq") * piece + jnp.arange(piece, dtype=jnp.int32)
    twist_re, twist_im = rotation(freq_index[:, None] * offsets[None, :], total, -1.0)
    twist_re = twist_re[:, :, None]
    twist_im = twist_im[:, :, None]
    turned_re = coarse_re * twist_re - coarse_im * twist_im
    turned_im = coarse_re * twist_im + coarse_im * twist_re
    moved = lax.all_to_all(
        jnp.stack([turned_re, turned_im]), "seq", split_axis=1, concat_axis=2, tiled=True
    )
    return local_forward(moved[0], moved[1])


def inverse_time(spec_re, spec_im, local_labels, all_labels):
    pairs, first, second, width = spec_re.shape
    rows = first * second
    steps = lax.axis_size("seq")
    double = 2 * steps
    total = double * rows
    time_re, time_im = local_inverse(spec_re, spec_im)
    positions = jnp.arange(rows, dtype=jnp.int32)
    twist_re, twist_im = rotation(local_labels[:, None] * positions[None, :], total, 1.0)
    twist_re = twist_re[:, :, None]
    twist_im = twist_im[:, :, None]
    turned_re = time_re * twist_re - time_im * twist_im
    turned_im = time_re * twist_im + time_im * twist_re
    moved = lax.all_to_all(
        jnp.stack([turned_re, turned_im]), "seq", split_axis=2, concat_axis=1, tiled=True
    )
    block_index = jnp.arange(steps, dtype=jnp.int32)
    table_re, table_im = rotation(block_index[:, None] * all_labels[None, :], double, 1.0)
    result_re = (
        contract("qk,krc->qrc", table_re, moved[0]) - contract("qk,krc->qrc", table_im, moved[1])
    ) / total
    result_im = (
        contract("qk,krc->qrc", table_re, moved[1]) + contract("qk,krc->qrc", table_im, moved[0])
    ) / total
    return (result_re, result_im)


def local(inputs, gate_values, out_grad, filter_taps, skip_gain):
    seq_input = inputs[0]
    seq_gate = gate_values[0]
    seq_grad = out_grad[0]
    rows, width = seq_input.shape
    replicas = lax.axis_size("dp")
    conv_grad = seq_grad * seq_gate
    spec_re, spec_im = forward_spectrum(
        jnp.concatenate([seq_input, conv_grad, filter_taps], axis=1)
    )
    filter_re = spec_re[..., 2 * width :]
    filter_im = spec_im[..., 2 * width :]
    input_re = spec_re[..., :width]
    input_im = spec_im[..., :width]
    grad_re = spec_re[..., width : 2 * width]
    grad_im = spec_im[..., width : 2 * width]
    conv_re = filter_re * input_re - filter_im * input_im
    conv_im = filter_re * input_im + filter_im * input_re
    corr_re = filter_re * grad_re + filter_im * grad_im
    corr_im = filter_re * grad_im - filter_im * grad_re
    taps_re = input_re * grad_re + input_im * grad_im
    taps_im = input_re * grad_im - input_im * grad_re
    packed_re = conv_re - corr_im
    packed_im = conv_im + corr_re
    local_labels, all_labels = frequency_labels()
    result_re, result_im = inverse_time(
        jnp.concatenate([packed_re, taps_re], axis=3),
        jnp.concatenate([packed_im, taps_im], axis=3),
        local_labels,
        all_labels,
    )
    results = jnp.concatenate([result_re, result_im[..., :width]], axis=2)
    timeline = lax.all_to_all(results, "seq", split_axis=0, concat_axis=1, tiled=True)[0]
    conv_time = timeline[:, :width]
    corr_time = timeline[:, timeline.shape[1] - width :]
    taps_time = timeline[:, width : timeline.shape[1] - width]
    taps_time = lax.psum_scatter(taps_time, "dp", scatter_dimension=1, tiled=True)
    gate_part = seq_grad * (conv_time + skip_gain[None, :] * seq_input)
    input_part = corr_time + skip_gain[None, :] * conv_grad
    length_total = rows * lax.axis_size("seq")
    batch_total = replicas * inputs.shape[0]
    filter_part = taps_time / math.sqrt(batch_total * length_total)
    return (input_part[None], gate_part[None], filter_part)


MESH = pl.DeviceIdType.MESH


def split_halves(table):
    high = table.astype(ml_dtypes.bfloat16)
    low = (table - high.astype(np.float64)).astype(ml_dtypes.bfloat16)
    return high, low


def block_tables(rows):
    double = 2 * rows
    place = np.arange(rows)
    turned = 2.0 * np.pi * ((place[:, None] * place[None, :]) % double) / double
    real = np.cos(turned)
    imag = -np.sin(turned)
    imag[:, 0] = 1.0 - 2.0 * (place % 2)
    forward = np.concatenate([real, imag], axis=1)
    weight = np.full((double, 1), 2.0 / double)
    weight[0] = weight[rows] = 1.0 / double
    inverse = forward.T * weight
    return split_halves(forward) + split_halves(inverse)


def dot3(values, high, low):
    top = values.astype(jnp.bfloat16)
    rest = (values - top.astype(jnp.float32)).astype(jnp.bfloat16)
    dot = functools.partial(jnp.dot, preferred_element_type=jnp.float32)
    return dot(top, high) + (dot(rest, high) + dot(top, low))


def kernel(
    steps, replicas, batch_total,
    in_any, gate_any, og_any, taps_any, skip_any, fh_any, fl_any, ih_any, il_any,
    ig_out, gg_out, fg_out,
    inp, gate, og, taps, skip, fh, fl, ih, il,
    sig, hsend, first_in, second_in, spec_first, spec_second, filt, prod, tprod,
    out_t, out_s, out_d, res, res_cross, res_taps,
    load_sem, h_send_sem, h_recv_sem, in_send_sem, in_recv_sem, out_send_sem, out_recv_sem,
    d_send_sem, d_recv_sem,
):
    devices = steps * replicas
    own_s = lax.axis_index("seq")
    own_d = lax.axis_index("dp")
    me = own_s * replicas + own_d
    rows, width = inp.shape
    lanes = 128
    half = steps // 2
    members = half * replicas
    side = own_s // half
    other = 1 - side
    place = me - members * side
    ahead = members // 2
    inner = jnp.where(side == 0, place >= ahead, place < ahead)
    cross_first = jnp.where(side == 0, 0, ahead)
    group = lax.rem(place + ahead, members)

    barrier = pltpu.get_barrier_semaphore()

    def greet(i, carry):
        p = lax.rem(me + i, devices)
        pl.semaphore_signal(
            barrier, inc=1, device_id=(p // replicas, lax.rem(p, replicas)), device_id_type=MESH
        )
        return carry

    loads = [
        pltpu.make_async_copy(src, dst, load_sem.at[k])
        for k, (src, dst) in enumerate([
            (taps_any, taps), (in_any, inp), (og_any, og), (gate_any, gate), (skip_any, skip),
            (fh_any, fh), (fl_any, fl), (ih_any, ih), (il_any, il),
        ])
    ]
    for copy in loads:
        copy.start()
    lax.fori_loop(1, devices, greet, 0)

    def remote(src, dst, src_sem, dst_sem, s, d):
        return pltpu.make_async_remote_copy(
            src_ref=src, dst_ref=dst, send_sem=src_sem, recv_sem=dst_sem,
            device_id=(s, d), device_id_type=MESH,
        )

    def arrived(ref, sem):
        pltpu.make_async_copy(ref, ref, sem).wait()

    def repeat(low, high, use):
        def body(i, carry):
            use(i)
            return carry

        lax.fori_loop(low, high, body, 0)

    def slot_of(block, of_side):
        return jnp.where(of_side == 0, steps - 1 - block, block)

    own_row = (slot_of(own_s, side) - half) * replicas + own_d
    cross_row = slot_of(own_s, other) * replicas + own_d
    h_row = lax.rem(own_s + half, steps)

    def group_at(s):
        return lax.rem(lax.rem(s, half) * replicas + own_d + ahead, members)

    h_low = jnp.where(side == 0, 0, half // 2)
    h_high = jnp.where(side == 0, steps, half + half // 2)

    def h_copy(s, sender):
        return remote(
            hsend.at[group_at(s)], first_in.at[h_row], h_send_sem.at[s], h_recv_sem.at[side], s, own_d
        )

    def h_each(use_remote, use_local):
        def body(s):
            @pl.when(s != own_s)
            def _():
                use_remote(s)

            if use_local is not None:
                @pl.when(s == own_s)
                def _():
                    use_local()

        repeat(h_low, h_high, body)

    def own_side(kind, which, dst_ref, base):
        def body(i):
            q = lax.rem(place + i, members)
            remote(
                sig.at[which, lax.rem(q + ahead, members)], dst_ref.at[base + own_row],
                in_send_sem.at[kind], in_recv_sem.at[kind],
                half * side + q // replicas, lax.rem(q, replicas),
            ).start()

        repeat(1, members, body)
        pltpu.make_async_copy(sig.at[which, group], dst_ref.at[base + own_row], in_recv_sem.at[kind]).start()

    def crossing():
        def body(i):
            q = jnp.where(side == 0, 0, ahead) + lax.rem(lax.rem(place, ahead) + i, ahead)
            remote(
                sig.at[side, lax.rem(q + ahead, members)], second_in.at[cross_row],
                in_send_sem.at[2], in_recv_sem.at[2],
                half * other + q // replicas, lax.rem(q, replicas),
            ).start()

        repeat(0, ahead, body)

    loads[0].wait()
    hsend[...] = taps[...].T.reshape(width // 8, 8, rows)
    loads[1].wait()
    sig[0] = inp[...].T.reshape(width // 8, 8, rows)
    loads[2].wait()
    loads[3].wait()
    gate[...] = og[...] * gate[...]
    sig[1] = gate[...].T.reshape(width // 8, 8, rows)
    pl.semaphore_wait(barrier, devices - 1)

    h_each(
        lambda s: h_copy(s, s).start(),
        lambda: pltpu.make_async_copy(hsend.at[group], first_in.at[h_row], h_recv_sem.at[side]).start(),
    )
    own_side(0, side, first_in, steps)
    crossing()
    own_side(1, other, second_in, members)

    for copy in loads[4:]:
        copy.wait()

    lane = lax.broadcasted_iota(jnp.int32, (8, lanes), 1)
    sign = (1 - 2 * lax.rem(lane, 2)).astype(jnp.float32)
    turn = jnp.where(side == 0, 1.0, -1.0).astype(jnp.float32)

    def slices(c):
        re_at = pl.ds(pl.multiple_of(c * lanes, lanes), lanes)
        im_at = pl.ds(pl.multiple_of(rows + c * lanes, lanes), lanes)
        return re_at, im_at, (lane + c * lanes) == 0

    def add(total, term):
        return term if total is None else total + term

    def h_at(j):
        return (j + half) % steps

    def send_own(source, base, kind, which):
        def body(i):
            q = lax.rem(place + i, members)
            s = half * side + q // replicas
            at = (slot_of(s, side) - half) * replicas + lax.rem(q, replicas)
            remote(
                source.at[base + at], res.at[which, group], out_send_sem.at[kind], out_recv_sem.at[kind],
                s, lax.rem(q, replicas),
            ).start()

        repeat(1, members, body)
        pltpu.make_async_copy(source.at[base + own_row], res.at[which, group], out_recv_sem.at[kind]).start()

    def send_cross():
        def body(i):
            q = lax.rem(place + i, members)
            s = half * other + q // replicas
            at = slot_of(s, side) * replicas + lax.rem(q, replicas)
            remote(
                out_t.at[at], res_cross.at[lax.rem(place, ahead)], out_send_sem.at[2], out_recv_sem.at[2],
                s, lax.rem(q, replicas),
            ).start()

        repeat(0, members, body)

    d_dst = group // (members // replicas)
    d_at = lax.rem(group, members // replicas)

    def d_each(count, use_remote, use_local):
        def body(i):
            u = lax.rem(own_s + i, count)
            to_self = jnp.logical_and(u == own_s, d_dst == own_d)
            to = jnp.where(u < half, side, 0)

            @pl.when(jnp.logical_not(to_self))
            def _():
                use_remote(remote(
                    out_d.at[u], res_taps.at[to, d_at], d_send_sem.at[u], d_recv_sem, u, d_dst
                ))

            if use_local:
                @pl.when(to_self)
                def _():
                    pltpu.make_async_copy(out_d.at[u], res_taps.at[to, d_at], d_recv_sem).start()

        repeat(0, count, body)

    def work(low):
        count = steps - low
        arrived(first_in.at[pl.ds(half, half)], h_recv_sem.at[0])
        if low == 0:
            arrived(first_in.at[pl.ds(0, half)], h_recv_sem.at[1])
        arrived(first_in.at[pl.ds(steps, members)], in_recv_sem.at[0])
        size = steps + members - low
        spec_first[pl.ds(low, size)] = dot3(
            first_in[pl.ds(low, size)].reshape(size * 8, rows), fh[...], fl[...]
        ).reshape(size, 8, 2 * rows)

        def prepare(c):
            re_at, im_at, first = slices(c)
            re = [spec_first[h_at(j), :, re_at] for j in range(count)]
            im = [spec_first[h_at(j), :, im_at] for j in range(count)]
            for j in range(count):
                out_re = re[j] if j == 0 else re[j] + sign * re[j - 1]
                out_im = im[j] if j == 0 else im[j] + sign * im[j - 1]
                filt[0, j, :, re_at] = out_re
                filt[1, j, :, re_at] = jnp.where(first, 0.0, turn * out_im)
                filt[2, j, :, re_at] = jnp.where(first, out_im, out_re)

        repeat(0, rows // lanes, prepare)

        def filters(re_at):
            return [[filt[i, j, :, re_at] for j in range(count)] for i in range(3)]

        def first_products(i):
            c, k = i // replicas, lax.rem(i, replicas)
            re_at, im_at, _ = slices(c)
            h_re, h_im, h_re2 = filters(re_at)
            t_re = [spec_first[steps + v * replicas + k, :, re_at] for v in range(half)]
            t_im = [spec_first[steps + v * replicas + k, :, im_at] for v in range(half)]
            for u in range(low, steps):
                re, im = None, None
                for v in range(max(u, half), steps):
                    j, w = v - u, v - half
                    re = add(re, h_re[j] * t_re[w] - h_im[j] * t_im[w])
                    im = add(im, h_re2[j] * t_im[w] + h_im[j] * t_re[w])
                prod[u * replicas + k, :, re_at] = re
                prod[u * replicas + k, :, im_at] = im

        repeat(0, rows // lanes * replicas, first_products)

        def inverse(source, start, size):
            return dot3(
                source[pl.ds(start, size)].reshape(size * 8, 2 * rows), ih[...], il[...]
            ).reshape(size, 8, rows)

        if low == 0:
            out_t[pl.ds(0, members)] = inverse(prod, 0, members)
            send_cross()
        out_t[pl.ds(members, members)] = inverse(prod, members, members)
        send_own(out_t, members, 0, side)

        arrived(second_in.at[pl.ds(members, members)], in_recv_sem.at[1])
        if low == 0:
            arrived(second_in.at[pl.ds(0, members)], in_recv_sem.at[2])
        start, size = low * replicas, count * replicas
        spec_second[pl.ds(start, size)] = dot3(
            second_in[pl.ds(start, size)].reshape(size * 8, rows), fh[...], fl[...]
        ).reshape(size, 8, 2 * rows)

        def second_products(i):
            c, k = i // replicas, lax.rem(i, replicas)
            re_at, im_at, _ = slices(c)
            h_re, h_im, h_re2 = filters(re_at)
            s_re = [spec_second[v * replicas + k, :, re_at] for v in range(low, steps)]
            s_im = [spec_second[v * replicas + k, :, im_at] for v in range(low, steps)]
            for u in range(half, steps):
                re, im = None, None
                for v in range(low, u + 1):
                    j, w = u - v, v - low
                    re = add(re, h_re[j] * s_re[w] + h_im[j] * s_im[w])
                    im = add(im, h_re2[j] * s_im[w] - h_im[j] * s_re[w])
                prod[(u - half) * replicas + k, :, re_at] = re
                prod[(u - half) * replicas + k, :, im_at] = im

        repeat(0, rows // lanes * replicas, second_products)
        out_s[...] = inverse(prod, 0, members)
        send_own(out_s, 0, 1, other)

        def taps_products(c):
            re_at, im_at, first = slices(c)
            flip = jnp.where(first, 1.0, -turn)
            sums_re, sums_im = [None] * count, [None] * count
            for k in range(replicas):
                t_re = [spec_first[steps + v * replicas + k, :, re_at] for v in range(half)]
                t_im = [spec_first[steps + v * replicas + k, :, im_at] for v in range(half)]
                for s in range(low, steps):
                    s_re = spec_second[s * replicas + k, :, re_at]
                    s_im = spec_second[s * replicas + k, :, im_at]
                    s_re2 = jnp.where(first, s_im, s_re)
                    s_im = jnp.where(first, 0.0, s_im)
                    for v in range(max(s, half), steps):
                        m, w = v - s, v - half
                        sums_re[m] = add(sums_re[m], t_re[w] * s_re + t_im[w] * s_im)
                        sums_im[m] = add(sums_im[m], t_im[w] * s_re2 - t_re[w] * s_im)
            for m in range(count):
                last = m == count - 1
                tprod[m, :, re_at] = sums_re[m] if last else sums_re[m] + sign * sums_re[m + 1]
                tprod[m, :, im_at] = flip * (sums_im[m] if last else sums_im[m] + sign * sums_im[m + 1])

        repeat(0, rows // lanes, taps_products)
        out_d[pl.ds(0, count)] = inverse(tprod, 0, count)
        d_each(count, lambda copy: copy.start(), True)

    pl.when(inner)(lambda: work(0))
    pl.when(jnp.logical_not(inner))(lambda: work(half))

    gain = skip[...]

    def positions(which):
        return res[which].reshape(width, rows).T

    def finish(is_second):
        ranges = pl.ds(0, ahead) if is_second else pl.ds(ahead, ahead)
        arrived(res.at[1 if is_second else 0], out_recv_sem.at[0])
        if is_second:
            ig_out[...] = positions(1) + gain * gate[...]
        else:
            gg_out[...] = og[...] * (positions(0) + gain * inp[...])
        late = 0 if is_second else 1
        arrived(res_cross, out_recv_sem.at[2])
        arrived(res.at[late], out_recv_sem.at[1])
        res[late, ranges] = res[late, ranges] + res_cross[...]
        if is_second:
            gg_out[...] = og[...] * (positions(0) + gain * inp[...])
        else:
            ig_out[...] = positions(1) + gain * gate[...]
        scale = 1.0 / math.sqrt(batch_total * rows * steps)
        if is_second:
            arrived(res_taps.at[0], d_recv_sem)
            total = res_taps[0]
        else:
            arrived(res_taps, d_recv_sem)
            total = res_taps[0] + res_taps[1]
        fg_out[...] = scale * total.reshape(width // replicas, rows)

    pl.when(side == 0)(lambda: finish(False))
    pl.when(side == 1)(lambda: finish(True))

    h_each(lambda s: h_copy(s, s).wait_send(), None)
    arrived(sig.at[0, pl.ds(0, members - 1)], in_send_sem.at[0])
    arrived(sig.at[0, pl.ds(0, members - 1)], in_send_sem.at[1])
    arrived(sig.at[0, pl.ds(0, ahead)], in_send_sem.at[2])
    arrived(sig.at[0, pl.ds(0, members - 1)], out_send_sem.at[0])
    arrived(sig.at[0, pl.ds(0, members - 1)], out_send_sem.at[1])

    @pl.when(inner)
    def _():
        arrived(sig.at[0], out_send_sem.at[2])
        d_each(steps, lambda copy: copy.wait_send(), False)

    @pl.when(jnp.logical_not(inner))
    def _():
        d_each(half, lambda copy: copy.wait_send(), False)


def hand_over(*refs):
    writes = [pltpu.make_async_copy(refs[k], refs[3 + k], refs[6].at[k]) for k in range(3)]
    for copy in writes:
        copy.start()
    for copy in writes:
        copy.wait()


def fused(inputs, gate_values, out_grad, filter_taps, skip_gain, steps, replicas):
    rows, width = filter_taps.shape
    double = 2 * rows
    members = steps * replicas // 2
    tables = block_tables(rows)
    f32, bf16 = jnp.float32, jnp.bfloat16
    dma = pltpu.SemaphoreType.DMA
    anywhere = pl.BlockSpec(memory_space=pltpu.HBM)
    near = pl.BlockSpec(memory_space=pltpu.VMEM)
    block = pltpu.VMEM((rows, width), f32)

    def tiles(*shape):
        return pltpu.VMEM(shape + (8, rows), f32)

    def spectra(count):
        return pltpu.VMEM((count, 8, double), f32)

    results = pl.pallas_call(
        functools.partial(kernel, steps, replicas, replicas * inputs.shape[0]),
        out_shape=(
            pltpu.VMEM((rows, width), f32),
            pltpu.VMEM((rows, width), f32),
            pltpu.VMEM((width // replicas, rows), f32),
        ),
        in_specs=[anywhere] * 9,
        out_specs=(near, near, near),
        scratch_shapes=[block, block, block, block, pltpu.VMEM((1, width), f32)]
        + [pltpu.VMEM((rows, double), bf16)] * 2
        + [pltpu.VMEM((double, rows), bf16)] * 2
        + [tiles(2, width // 8), tiles(width // 8), tiles(steps + members), tiles(2 * members)]
        + [spectra(steps + members), spectra(2 * members), tiles(3, steps)]
        + [spectra(2 * members), spectra(steps)]
        + [tiles(2 * members), tiles(members), tiles(steps)]
        + [tiles(2, width // 8), tiles(width // 16), tiles(2, width // 8 // replicas)]
        + [dma((9,)), dma((steps,)), dma((2,)), dma((3,)), dma((3,)), dma((3,)), dma((3,)), dma((steps,)), dma]
        ,
        compiler_params=pltpu.CompilerParams(
            collective_id=0, has_side_effects=True, vmem_limit_bytes=48 * 1024 * 1024
        ),
    )(
        *[
            pltpu.with_memory_space_constraint(value, pltpu.HBM)
            for value in (
                inputs[0], gate_values[0], out_grad[0], filter_taps, skip_gain[None, :],
                *[jnp.asarray(table) for table in tables],
            )
        ],
    )
    input_part, gate_part, filter_part = pl.pallas_call(
        hand_over,
        out_shape=tuple(jax.ShapeDtypeStruct(part.shape, part.dtype) for part in results),
        in_specs=[near] * 3,
        out_specs=(anywhere,) * 3,
        scratch_shapes=[dma((3,))],
        compiler_params=pltpu.CompilerParams(vmem_limit_bytes=2 * 1024 * 1024),
    )(*results)
    return input_part[None], gate_part[None], filter_part.T


def solution(mesh):
    placed = (P("dp", "seq", None), P("dp", "seq", None), P("dp", "seq", None), P("seq", None), P())
    steps, replicas = mesh.shape["seq"], mesh.shape["dp"]

    def either(inputs, gate_values, out_grad, filter_taps, skip_gain):
        rows, width = filter_taps.shape
        fits = width == 128 and (steps, replicas) == (8, 4) and rows % 128 == 0
        if fits and inputs.shape[0] == 1:
            return fused(inputs, gate_values, out_grad, filter_taps, skip_gain, steps, replicas)
        return local(inputs, gate_values, out_grad, filter_taps, skip_gain)

    return jax.shard_map(
        either,
        mesh=mesh,
        in_specs=placed,
        out_specs=(P("dp", "seq", None), P("dp", "seq", None), P("seq", "dp")),
        check_vma=False,
    )
```

```python
import functools
import math

import jax
import jax.numpy as jnp
import ml_dtypes
import numpy as np
from jax import lax
from jax.experimental import pallas as pl
from jax.experimental.pallas import tpu as pltpu
from jax.sharding import PartitionSpec as P

first_radix = 32


def rotation(product, modulus, direction):
    fraction = (product % modulus).astype(jnp.float32) / modulus
    turned = 2.0 * math.pi * fraction
    return (jnp.cos(turned), direction * jnp.sin(turned))


def contract(formula, matrix, operand):
    return jnp.einsum(
        formula,
        matrix,
        operand,
        precision=lax.Precision.HIGHEST,
        preferred_element_type=jnp.float32,
    )


def complex_apply(formula, table_re, table_im, values_re, values_im):
    result_re = contract(formula, table_re, values_re) - contract(formula, table_im, values_im)
    result_im = contract(formula, table_re, values_im) + contract(formula, table_im, values_re)
    return (result_re, result_im)


def local_forward(values_re, values_im):
    pairs, rows, width = values_re.shape
    second = rows // first_radix
    values_re = values_re.reshape(pairs, first_radix, second, width)
    values_im = values_im.reshape(pairs, first_radix, second, width)
    outer = jnp.arange(first_radix, dtype=jnp.int32)
    inner = jnp.arange(second, dtype=jnp.int32)
    table_re, table_im = rotation(outer[:, None] * outer[None, :], first_radix, -1.0)
    section_re, section_im = complex_apply(
        "ca,mabx->mcbx", table_re, table_im, values_re, values_im
    )
    twist_re, twist_im = rotation(outer[:, None] * inner[None, :], rows, -1.0)
    twist_re = twist_re[None, :, :, None]
    twist_im = twist_im[None, :, :, None]
    turned_re = section_re * twist_re - section_im * twist_im
    turned_im = section_re * twist_im + section_im * twist_re
    table_re, table_im = rotation(inner[:, None] * inner[None, :], second, -1.0)
    return complex_apply("db,mcbx->mcdx", table_re, table_im, turned_re, turned_im)


def local_inverse(spec_re, spec_im):
    pairs, first, second, width = spec_re.shape
    rows = first * second
    outer = jnp.arange(first, dtype=jnp.int32)
    inner = jnp.arange(second, dtype=jnp.int32)
    table_re, table_im = rotation(inner[:, None] * inner[None, :], second, 1.0)
    section_re, section_im = complex_apply("bd,mcdx->mcbx", table_re, table_im, spec_re, spec_im)
    twist_re, twist_im = rotation(outer[:, None] * inner[None, :], rows, 1.0)
    twist_re = twist_re[None, :, :, None]
    twist_im = twist_im[None, :, :, None]
    turned_re = section_re * twist_re - section_im * twist_im
    turned_im = section_re * twist_im + section_im * twist_re
    table_re, table_im = rotation(outer[:, None] * outer[None, :], first, 1.0)
    result_re, result_im = complex_apply("ac,mcbx->mabx", table_re, table_im, turned_re, turned_im)
    return (result_re.reshape(pairs, rows, width), result_im.reshape(pairs, rows, width))


def frequency_labels():
    steps = lax.axis_size("seq")
    own = lax.axis_index("seq")
    local_labels = 2 * own + jnp.arange(2, dtype=jnp.int32)
    all_labels = jnp.arange(2 * steps, dtype=jnp.int32)
    return (local_labels, all_labels)


def forward_spectrum(signal):
    rows, width = signal.shape
    steps = lax.axis_size("seq")
    piece = rows // steps
    double = 2 * steps
    total = double * rows
    columns = lax.all_to_all(
        signal.reshape(1, rows, width), "seq", split_axis=1, concat_axis=0, tiled=True
    )
    block_index = jnp.arange(steps, dtype=jnp.int32)
    freq_index = jnp.arange(double, dtype=jnp.int32)
    table_re, table_im = rotation(freq_index[:, None] * block_index[None, :], double, -1.0)
    coarse_re = contract("kq,qrc->krc", table_re, columns)
    coarse_im = contract("kq,qrc->krc", table_im, columns)
    offsets = lax.axis_index("seq") * piece + jnp.arange(piece, dtype=jnp.int32)
    twist_re, twist_im = rotation(freq_index[:, None] * offsets[None, :], total, -1.0)
    twist_re = twist_re[:, :, None]
    twist_im = twist_im[:, :, None]
    turned_re = coarse_re * twist_re - coarse_im * twist_im
    turned_im = coarse_re * twist_im + coarse_im * twist_re
    moved = lax.all_to_all(
        jnp.stack([turned_re, turned_im]), "seq", split_axis=1, concat_axis=2, tiled=True
    )
    return local_forward(moved[0], moved[1])


def inverse_time(spec_re, spec_im, local_labels, all_labels):
    pairs, first, second, width = spec_re.shape
    rows = first * second
    steps = lax.axis_size("seq")
    double = 2 * steps
    total = double * rows
    time_re, time_im = local_inverse(spec_re, spec_im)
    positions = jnp.arange(rows, dtype=jnp.int32)
    twist_re, twist_im = rotation(local_labels[:, None] * positions[None, :], total, 1.0)
    twist_re = twist_re[:, :, None]
    twist_im = twist_im[:, :, None]
    turned_re = time_re * twist_re - time_im * twist_im
    turned_im = time_re * twist_im + time_im * twist_re
    moved = lax.all_to_all(
        jnp.stack([turned_re, turned_im]), "seq", split_axis=2, concat_axis=1, tiled=True
    )
    block_index = jnp.arange(steps, dtype=jnp.int32)
    table_re, table_im = rotation(block_index[:, None] * all_labels[None, :], double, 1.0)
    result_re = (
        contract("qk,krc->qrc", table_re, moved[0]) - contract("qk,krc->qrc", table_im, moved[1])
    ) / total
    result_im = (
        contract("qk,krc->qrc", table_re, moved[1]) + contract("qk,krc->qrc", table_im, moved[0])
    ) / total
    return (result_re, result_im)


def local(inputs, gate_values, out_grad, filter_taps, skip_gain):
    seq_input = inputs[0]
    seq_gate = gate_values[0]
    seq_grad = out_grad[0]
    rows, width = seq_input.shape
    replicas = lax.axis_size("dp")
    conv_grad = seq_grad * seq_gate
    spec_re, spec_im = forward_spectrum(
        jnp.concatenate([seq_input, conv_grad, filter_taps], axis=1)
    )
    filter_re = spec_re[..., 2 * width :]
    filter_im = spec_im[..., 2 * width :]
    input_re = spec_re[..., :width]
    input_im = spec_im[..., :width]
    grad_re = spec_re[..., width : 2 * width]
    grad_im = spec_im[..., width : 2 * width]
    conv_re = filter_re * input_re - filter_im * input_im
    conv_im = filter_re * input_im + filter_im * input_re
    corr_re = filter_re * grad_re + filter_im * grad_im
    corr_im = filter_re * grad_im - filter_im * grad_re
    taps_re = input_re * grad_re + input_im * grad_im
    taps_im = input_re * grad_im - input_im * grad_re
    packed_re = conv_re - corr_im
    packed_im = conv_im + corr_re
    local_labels, all_labels = frequency_labels()
    result_re, result_im = inverse_time(
        jnp.concatenate([packed_re, taps_re], axis=3),
        jnp.concatenate([packed_im, taps_im], axis=3),
        local_labels,
        all_labels,
    )
    results = jnp.concatenate([result_re, result_im[..., :width]], axis=2)
    timeline = lax.all_to_all(results, "seq", split_axis=0, concat_axis=1, tiled=True)[0]
    conv_time = timeline[:, :width]
    corr_time = timeline[:, timeline.shape[1] - width :]
    taps_time = timeline[:, width : timeline.shape[1] - width]
    taps_time = lax.psum_scatter(taps_time, "dp", scatter_dimension=1, tiled=True)
    gate_part = seq_grad * (conv_time + skip_gain[None, :] * seq_input)
    input_part = corr_time + skip_gain[None, :] * conv_grad
    length_total = rows * lax.axis_size("seq")
    batch_total = replicas * inputs.shape[0]
    filter_part = taps_time / math.sqrt(batch_total * length_total)
    return (input_part[None], gate_part[None], filter_part)


MESH = pl.DeviceIdType.MESH


def split_halves(table):
    high = table.astype(ml_dtypes.bfloat16)
    low = (table - high.astype(np.float64)).astype(ml_dtypes.bfloat16)
    return high, low


def block_tables(rows):
    double = 2 * rows
    place = np.arange(rows)
    turned = 2.0 * np.pi * ((place[:, None] * place[None, :]) % double) / double
    real = np.cos(turned)
    imag = -np.sin(turned)
    imag[:, 0] = 1.0 - 2.0 * (place % 2)
    forward = np.concatenate([real, imag], axis=1)
    weight = np.full((double, 1), 2.0 / double)
    weight[0] = weight[rows] = 1.0 / double
    inverse = forward.T * weight
    return split_halves(forward) + split_halves(inverse)


def dot3(values, high, low):
    top = values.astype(jnp.bfloat16)
    rest = (values - top.astype(jnp.float32)).astype(jnp.bfloat16)
    dot = functools.partial(jnp.dot, preferred_element_type=jnp.float32)
    return dot(top, high) + (dot(rest, high) + dot(top, low))


def kernel(
    steps, replicas, batch_total,
    in_any, gate_any, og_any, taps_any, skip_any, fh_any, fl_any, ih_any, il_any,
    ig_out, gg_out, fg_out,
    inp, gate, og, taps, skip, fh, fl, ih, il,
    sig, hsend, first_in, second_in, spec_first, spec_second, filt, prod, tprod,
    out_t, out_s, out_d, res, res_cross, res_taps, part,
    load_sem, h_send_sem, h_recv_sem, in_send_sem, in_recv_sem, out_send_sem, out_recv_sem,
    d_send_sem, d_recv_sem,
):
    devices = steps * replicas
    own_s = lax.axis_index("seq")
    own_d = lax.axis_index("dp")
    me = own_s * replicas + own_d
    rows, width = inp.shape
    lanes = 128
    half = steps // 2
    members = half * replicas
    side = own_s // half
    other = 1 - side
    place = me - members * side
    ahead = members // 2
    inner = jnp.where(side == 0, place >= ahead, place < ahead)
    cross_first = jnp.where(side == 0, 0, ahead)
    group = lax.rem(place + ahead, members)

    barrier = pltpu.get_barrier_semaphore()

    def greet(i, carry):
        p = lax.rem(me + i, devices)
        pl.semaphore_signal(
            barrier, inc=1, device_id=(p // replicas, lax.rem(p, replicas)), device_id_type=MESH
        )
        return carry

    loads = [
        pltpu.make_async_copy(src, dst, load_sem.at[k])
        for k, (src, dst) in enumerate([
            (taps_any, taps), (in_any, inp), (og_any, og), (gate_any, gate), (skip_any, skip),
            (fh_any, fh), (fl_any, fl), (ih_any, ih), (il_any, il),
        ])
    ]
    for copy in loads:
        copy.start()
    lax.fori_loop(1, devices, greet, 0)

    def remote(src, dst, src_sem, dst_sem, s, d):
        return pltpu.make_async_remote_copy(
            src_ref=src, dst_ref=dst, send_sem=src_sem, recv_sem=dst_sem,
            device_id=(s, d), device_id_type=MESH,
        )

    def arrived(ref, sem):
        pltpu.make_async_copy(ref, ref, sem).wait()

    def repeat(low, high, use):
        def body(i, carry):
            use(i)
            return carry

        lax.fori_loop(low, high, body, 0)

    def slot_of(block, of_side):
        return jnp.where(of_side == 0, steps - 1 - block, block)

    own_row = (slot_of(own_s, side) - half) * replicas + own_d
    cross_row = slot_of(own_s, other) * replicas + own_d
    h_row = lax.rem(own_s + half, steps)

    def group_at(s):
        return lax.rem(lax.rem(s, half) * replicas + own_d + ahead, members)

    h_low = jnp.where(side == 0, 0, half // 2)
    h_high = jnp.where(side == 0, steps, half + half // 2)

    def h_copy(s, sender):
        return remote(
            hsend.at[group_at(s)], first_in.at[h_row], h_send_sem.at[s], h_recv_sem.at[side], s, own_d
        )

    def h_each(use_remote, use_local):
        def body(s):
            @pl.when(s != own_s)
            def _():
                use_remote(s)

            if use_local is not None:
                @pl.when(s == own_s)
                def _():
                    use_local()

        repeat(h_low, h_high, body)

    def own_side(kind, which, dst_ref, base):
        def body(i):
            q = lax.rem(place + i, members)
            remote(
                sig.at[which, lax.rem(q + ahead, members)], dst_ref.at[base + own_row],
                in_send_sem.at[kind], in_recv_sem.at[kind],
                half * side + q // replicas, lax.rem(q, replicas),
            ).start()

        repeat(1, members, body)
        pltpu.make_async_copy(sig.at[which, group], dst_ref.at[base + own_row], in_recv_sem.at[kind]).start()

    def crossing():
        def body(i):
            q = jnp.where(side == 0, 0, ahead) + lax.rem(lax.rem(place, ahead) + i, ahead)
            remote(
                sig.at[side, lax.rem(q + ahead, members)], second_in.at[cross_row],
                in_send_sem.at[2], in_recv_sem.at[2],
                half * other + q // replicas, lax.rem(q, replicas),
            ).start()

        repeat(0, ahead, body)

    def prepare_input():
        loads[1].wait()
        sig[0] = inp[...].T.reshape(width // 8, 8, rows)

    def prepare_grad():
        loads[2].wait()
        loads[3].wait()
        gate[...] = og[...] * gate[...]
        sig[1] = gate[...].T.reshape(width // 8, 8, rows)

    loads[0].wait()
    hsend[...] = taps[...].T.reshape(width // 8, 8, rows)
    pl.when(side == 0)(prepare_input)
    pl.when(side == 1)(prepare_grad)
    pl.semaphore_wait(barrier, devices - 1)
    h_each(
        lambda s: h_copy(s, s).start(),
        lambda: pltpu.make_async_copy(hsend.at[group], first_in.at[h_row], h_recv_sem.at[side]).start(),
    )
    own_side(0, side, first_in, steps)
    crossing()
    pl.when(side == 0)(prepare_grad)
    pl.when(side == 1)(prepare_input)
    own_side(1, other, second_in, members)

    for copy in loads[4:]:
        copy.wait()

    lane = lax.broadcasted_iota(jnp.int32, (8, lanes), 1)
    sign = (1 - 2 * lax.rem(lane, 2)).astype(jnp.float32)
    turn = jnp.where(side == 0, 1.0, -1.0).astype(jnp.float32)

    def slices(c):
        re_at = pl.ds(pl.multiple_of(c * lanes, lanes), lanes)
        im_at = pl.ds(pl.multiple_of(rows + c * lanes, lanes), lanes)
        return re_at, im_at, (lane + c * lanes) == 0

    def add(total, term):
        return term if total is None else total + term

    def h_at(j):
        return (j + half) % steps

    def send_own(source, base, kind, which):
        def body(i):
            q = lax.rem(place + i, members)
            s = half * side + q // replicas
            at = (slot_of(s, side) - half) * replicas + lax.rem(q, replicas)
            remote(
                source.at[base + at], res.at[which, group], out_send_sem.at[kind], out_recv_sem.at[kind],
                s, lax.rem(q, replicas),
            ).start()

        repeat(1, members, body)
        pltpu.make_async_copy(source.at[base + own_row], res.at[which, group], out_recv_sem.at[kind]).start()

    def send_cross():
        def body(i):
            q = lax.rem(place + i, members)
            s = half * other + q // replicas
            at = slot_of(s, side) * replicas + lax.rem(q, replicas)
            remote(
                out_t.at[at], res_cross.at[lax.rem(place, ahead)], out_send_sem.at[2], out_recv_sem.at[2],
                s, lax.rem(q, replicas),
            ).start()

        repeat(0, members, body)

    d_dst = group // (members // replicas)
    d_at = lax.rem(group, members // replicas)

    def d_each(use_remote, use_local):
        def body(i):
            u = lax.rem(own_s + i, steps)
            to_self = jnp.logical_and(u == own_s, d_dst == own_d)

            @pl.when(jnp.logical_not(to_self))
            def _():
                use_remote(remote(
                    out_d.at[u], res_taps.at[d_at], d_send_sem.at[u], d_recv_sem.at[0], u, d_dst
                ))

            if use_local:
                @pl.when(to_self)
                def _():
                    pltpu.make_async_copy(out_d.at[u], res_taps.at[d_at], d_recv_sem.at[0]).start()

        repeat(0, steps, body)

    def part_copy():
        return remote(
            out_d.at[pl.ds(0, half)], part, d_send_sem.at[0], d_recv_sem.at[1],
            lax.rem(own_s + half, steps), own_d,
        )

    def work(low):
        count = steps - low
        def transform_first(start, size):
            spec_first[pl.ds(start, size)] = dot3(
                first_in[pl.ds(start, size)].reshape(size * 8, rows), fh[...], fl[...]
            ).reshape(size, 8, 2 * rows)

        arrived(first_in.at[pl.ds(half, half)], h_recv_sem.at[0])
        if low == 0:
            arrived(first_in.at[pl.ds(0, half)], h_recv_sem.at[1])
        transform_first(low, count)

        def prepare(c):
            re_at, im_at, first = slices(c)
            re = [spec_first[h_at(j), :, re_at] for j in range(count)]
            im = [spec_first[h_at(j), :, im_at] for j in range(count)]
            for j in range(count):
                out_re = re[j] if j == 0 else re[j] + sign * re[j - 1]
                out_im = im[j] if j == 0 else im[j] + sign * im[j - 1]
                filt[0, j, :, re_at] = out_re
                filt[1, j, :, re_at] = jnp.where(first, 0.0, turn * out_im)
                filt[2, j, :, re_at] = jnp.where(first, out_im, out_re)

        repeat(0, rows // lanes, prepare)
        arrived(first_in.at[pl.ds(steps, members)], in_recv_sem.at[0])
        transform_first(steps, members)

        def filters(re_at):
            return [[filt[i, j, :, re_at] for j in range(count)] for i in range(3)]

        def first_products(i):
            c, k = i // replicas, lax.rem(i, replicas)
            re_at, im_at, _ = slices(c)
            h_re, h_im, h_re2 = filters(re_at)
            t_re = [spec_first[steps + v * replicas + k, :, re_at] for v in range(half)]
            t_im = [spec_first[steps + v * replicas + k, :, im_at] for v in range(half)]
            for u in range(low, steps):
                re, im = None, None
                for v in range(max(u, half), steps):
                    j, w = v - u, v - half
                    re = add(re, h_re[j] * t_re[w] - h_im[j] * t_im[w])
                    im = add(im, h_re2[j] * t_im[w] + h_im[j] * t_re[w])
                prod[u * replicas + k, :, re_at] = re
                prod[u * replicas + k, :, im_at] = im

        repeat(0, rows // lanes * replicas, first_products)

        def inverse(source, start, size):
            return dot3(
                source[pl.ds(start, size)].reshape(size * 8, 2 * rows), ih[...], il[...]
            ).reshape(size, 8, rows)

        if low == 0:
            out_t[pl.ds(0, members)] = inverse(prod, 0, members)
            send_cross()
        out_t[pl.ds(members, members)] = inverse(prod, members, members)
        send_own(out_t, members, 0, side)

        def transform(start):
            spec_second[pl.ds(start, members)] = dot3(
                second_in[pl.ds(start, members)].reshape(members * 8, rows), fh[...], fl[...]
            ).reshape(members, 8, 2 * rows)

        if low == 0:
            arrived(second_in.at[pl.ds(0, members)], in_recv_sem.at[2])
            transform(0)
        arrived(second_in.at[pl.ds(members, members)], in_recv_sem.at[1])
        transform(members)

        def second_products(i):
            c, k = i // replicas, lax.rem(i, replicas)
            re_at, im_at, _ = slices(c)
            h_re, h_im, h_re2 = filters(re_at)
            s_re = [spec_second[v * replicas + k, :, re_at] for v in range(low, steps)]
            s_im = [spec_second[v * replicas + k, :, im_at] for v in range(low, steps)]
            for u in range(half, steps):
                re, im = None, None
                for v in range(low, u + 1):
                    j, w = u - v, v - low
                    re = add(re, h_re[j] * s_re[w] + h_im[j] * s_im[w])
                    im = add(im, h_re2[j] * s_im[w] - h_im[j] * s_re[w])
                prod[(u - half) * replicas + k, :, re_at] = re
                prod[(u - half) * replicas + k, :, im_at] = im

        def taps_products(c):
            re_at, im_at, first = slices(c)
            flip = jnp.where(first, 1.0, -turn)
            sums_re, sums_im = [None] * count, [None] * count
            for k in range(replicas):
                t_re = [spec_first[steps + v * replicas + k, :, re_at] for v in range(half)]
                t_im = [spec_first[steps + v * replicas + k, :, im_at] for v in range(half)]
                for s in range(low, steps):
                    s_re = spec_second[s * replicas + k, :, re_at]
                    s_im = spec_second[s * replicas + k, :, im_at]
                    s_re2 = jnp.where(first, s_im, s_re)
                    s_im = jnp.where(first, 0.0, s_im)
                    for v in range(max(s, half), steps):
                        m, w = v - s, v - half
                        sums_re[m] = add(sums_re[m], t_re[w] * s_re + t_im[w] * s_im)
                        sums_im[m] = add(sums_im[m], t_im[w] * s_re2 - t_re[w] * s_im)
            for m in range(count):
                last = m == count - 1
                tprod[m, :, re_at] = sums_re[m] if last else sums_re[m] + sign * sums_re[m + 1]
                tprod[m, :, im_at] = flip * (sums_im[m] if last else sums_im[m] + sign * sums_im[m + 1])

        def finish_second():
            repeat(0, rows // lanes * replicas, second_products)
            out_s[...] = inverse(prod, 0, members)
            send_own(out_s, 0, 1, other)

        def finish_taps():
            repeat(0, rows // lanes, taps_products)
            out_d[pl.ds(0, count)] = inverse(tprod, 0, count)
            if low == 0:
                arrived(part, d_recv_sem.at[1])
                out_d[pl.ds(0, half)] = out_d[pl.ds(0, half)] + part[...]
                d_each(lambda copy: copy.start(), True)
            else:
                part_copy().start()

        if low == 0:
            finish_second()
            finish_taps()
        else:
            finish_taps()
            finish_second()

    pl.when(inner)(lambda: work(0))
    pl.when(jnp.logical_not(inner))(lambda: work(half))

    gain = skip[...]

    def positions(which):
        return res[which].reshape(width, rows).T

    def finish(is_second):
        ranges = pl.ds(0, ahead) if is_second else pl.ds(ahead, ahead)
        arrived(res.at[1 if is_second else 0], out_recv_sem.at[0])
        if is_second:
            ig_out[...] = positions(1) + gain * gate[...]
        else:
            gg_out[...] = og[...] * (positions(0) + gain * inp[...])
        late = 0 if is_second else 1
        arrived(res_cross, out_recv_sem.at[2])
        arrived(res.at[late], out_recv_sem.at[1])
        res[late, ranges] = res[late, ranges] + res_cross[...]
        if is_second:
            gg_out[...] = og[...] * (positions(0) + gain * inp[...])
        else:
            ig_out[...] = positions(1) + gain * gate[...]
        scale = 1.0 / math.sqrt(batch_total * rows * steps)
        arrived(res_taps, d_recv_sem.at[0])
        fg_out[...] = scale * res_taps[...].reshape(width // replicas, rows)

    pl.when(side == 0)(lambda: finish(False))
    pl.when(side == 1)(lambda: finish(True))

    h_each(lambda s: h_copy(s, s).wait_send(), None)
    arrived(sig.at[0, pl.ds(0, members - 1)], in_send_sem.at[0])
    arrived(sig.at[0, pl.ds(0, members - 1)], in_send_sem.at[1])
    arrived(sig.at[0, pl.ds(0, ahead)], in_send_sem.at[2])
    arrived(sig.at[0, pl.ds(0, members - 1)], out_send_sem.at[0])
    arrived(sig.at[0, pl.ds(0, members - 1)], out_send_sem.at[1])

    @pl.when(inner)
    def _():
        arrived(sig.at[0], out_send_sem.at[2])
        d_each(lambda copy: copy.wait_send(), False)

    @pl.when(jnp.logical_not(inner))
    def _():
        part_copy().wait_send()


def hand_over(*refs):
    writes = [pltpu.make_async_copy(refs[k], refs[3 + k], refs[6].at[k]) for k in range(3)]
    for copy in writes:
        copy.start()
    for copy in writes:
        copy.wait()


def fused(inputs, gate_values, out_grad, filter_taps, skip_gain, steps, replicas):
    rows, width = filter_taps.shape
    double = 2 * rows
    members = steps * replicas // 2
    tables = block_tables(rows)
    f32, bf16 = jnp.float32, jnp.bfloat16
    dma = pltpu.SemaphoreType.DMA
    anywhere = pl.BlockSpec(memory_space=pltpu.HBM)
    near = pl.BlockSpec(memory_space=pltpu.VMEM)
    block = pltpu.VMEM((rows, width), f32)

    def tiles(*shape):
        return pltpu.VMEM(shape + (8, rows), f32)

    def spectra(count):
        return pltpu.VMEM((count, 8, double), f32)

    results = pl.pallas_call(
        functools.partial(kernel, steps, replicas, replicas * inputs.shape[0]),
        out_shape=(
            pltpu.VMEM((rows, width), f32),
            pltpu.VMEM((rows, width), f32),
            pltpu.VMEM((width // replicas, rows), f32),
        ),
        in_specs=[anywhere] * 9,
        out_specs=(near, near, near),
        scratch_shapes=[block, block, block, block, pltpu.VMEM((1, width), f32)]
        + [pltpu.VMEM((rows, double), bf16)] * 2
        + [pltpu.VMEM((double, rows), bf16)] * 2
        + [tiles(2, width // 8), tiles(width // 8), tiles(steps + members), tiles(2 * members)]
        + [spectra(steps + members), spectra(2 * members), tiles(3, steps)]
        + [spectra(2 * members), spectra(steps)]
        + [tiles(2 * members), tiles(members), tiles(steps)]
        + [tiles(2, width // 8), tiles(width // 16), tiles(width // 8 // replicas), tiles(steps // 2)]
        + [dma((9,)), dma((steps,)), dma((2,)), dma((3,)), dma((3,)), dma((3,)), dma((3,)), dma((steps,)), dma((2,))],
        compiler_params=pltpu.CompilerParams(
            collective_id=0, has_side_effects=True, vmem_limit_bytes=48 * 1024 * 1024
        ),
    )(
        *[
            pltpu.with_memory_space_constraint(value, pltpu.HBM)
            for value in (
                inputs[0], gate_values[0], out_grad[0], filter_taps, skip_gain[None, :],
                *[jnp.asarray(table) for table in tables],
            )
        ],
    )
    input_part, gate_part, filter_part = pl.pallas_call(
        hand_over,
        out_shape=tuple(jax.ShapeDtypeStruct(part.shape, part.dtype) for part in results),
        in_specs=[near] * 3,
        out_specs=(anywhere,) * 3,
        scratch_shapes=[dma((3,))],
        compiler_params=pltpu.CompilerParams(vmem_limit_bytes=2 * 1024 * 1024),
    )(*results)
    return input_part[None], gate_part[None], filter_part.T


def solution(mesh):
    placed = (P("dp", "seq", None), P("dp", "seq", None), P("dp", "seq", None), P("seq", None), P())
    steps, replicas = mesh.shape["seq"], mesh.shape["dp"]

    def either(inputs, gate_values, out_grad, filter_taps, skip_gain):
        rows, width = filter_taps.shape
        fits = width == 128 and (steps, replicas) == (8, 4) and rows % 128 == 0
        if fits and inputs.shape[0] == 1:
            return fused(inputs, gate_values, out_grad, filter_taps, skip_gain, steps, replicas)
        return local(inputs, gate_values, out_grad, filter_taps, skip_gain)

    return jax.shard_map(
        either,
        mesh=mesh,
        in_specs=placed,
        out_specs=(P("dp", "seq", None), P("dp", "seq", None), P("seq", "dp")),
        check_vma=False,
    )
```

```python
import functools
import math

import jax
import jax.numpy as jnp
import ml_dtypes
import numpy as np
from jax import lax
from jax.experimental import pallas as pl
from jax.experimental.pallas import tpu as pltpu
from jax.sharding import PartitionSpec as P

first_radix = 32


def rotation(product, modulus, direction):
    fraction = (product % modulus).astype(jnp.float32) / modulus
    turned = 2.0 * math.pi * fraction
    return (jnp.cos(turned), direction * jnp.sin(turned))


def contract(formula, matrix, operand):
    return jnp.einsum(
        formula,
        matrix,
        operand,
        precision=lax.Precision.HIGHEST,
        preferred_element_type=jnp.float32,
    )


def complex_apply(formula, table_re, table_im, values_re, values_im):
    result_re = contract(formula, table_re, values_re) - contract(formula, table_im, values_im)
    result_im = contract(formula, table_re, values_im) + contract(formula, table_im, values_re)
    return (result_re, result_im)


def local_forward(values_re, values_im):
    pairs, rows, width = values_re.shape
    second = rows // first_radix
    values_re = values_re.reshape(pairs, first_radix, second, width)
    values_im = values_im.reshape(pairs, first_radix, second, width)
    outer = jnp.arange(first_radix, dtype=jnp.int32)
    inner = jnp.arange(second, dtype=jnp.int32)
    table_re, table_im = rotation(outer[:, None] * outer[None, :], first_radix, -1.0)
    section_re, section_im = complex_apply(
        "ca,mabx->mcbx", table_re, table_im, values_re, values_im
    )
    twist_re, twist_im = rotation(outer[:, None] * inner[None, :], rows, -1.0)
    twist_re = twist_re[None, :, :, None]
    twist_im = twist_im[None, :, :, None]
    turned_re = section_re * twist_re - section_im * twist_im
    turned_im = section_re * twist_im + section_im * twist_re
    table_re, table_im = rotation(inner[:, None] * inner[None, :], second, -1.0)
    return complex_apply("db,mcbx->mcdx", table_re, table_im, turned_re, turned_im)


def local_inverse(spec_re, spec_im):
    pairs, first, second, width = spec_re.shape
    rows = first * second
    outer = jnp.arange(first, dtype=jnp.int32)
    inner = jnp.arange(second, dtype=jnp.int32)
    table_re, table_im = rotation(inner[:, None] * inner[None, :], second, 1.0)
    section_re, section_im = complex_apply("bd,mcdx->mcbx", table_re, table_im, spec_re, spec_im)
    twist_re, twist_im = rotation(outer[:, None] * inner[None, :], rows, 1.0)
    twist_re = twist_re[None, :, :, None]
    twist_im = twist_im[None, :, :, None]
    turned_re = section_re * twist_re - section_im * twist_im
    turned_im = section_re * twist_im + section_im * twist_re
    table_re, table_im = rotation(outer[:, None] * outer[None, :], first, 1.0)
    result_re, result_im = complex_apply("ac,mcbx->mabx", table_re, table_im, turned_re, turned_im)
    return (result_re.reshape(pairs, rows, width), result_im.reshape(pairs, rows, width))


def frequency_labels():
    steps = lax.axis_size("seq")
    own = lax.axis_index("seq")
    local_labels = 2 * own + jnp.arange(2, dtype=jnp.int32)
    all_labels = jnp.arange(2 * steps, dtype=jnp.int32)
    return (local_labels, all_labels)


def forward_spectrum(signal):
    rows, width = signal.shape
    steps = lax.axis_size("seq")
    piece = rows // steps
    double = 2 * steps
    total = double * rows
    columns = lax.all_to_all(
        signal.reshape(1, rows, width), "seq", split_axis=1, concat_axis=0, tiled=True
    )
    block_index = jnp.arange(steps, dtype=jnp.int32)
    freq_index = jnp.arange(double, dtype=jnp.int32)
    table_re, table_im = rotation(freq_index[:, None] * block_index[None, :], double, -1.0)
    coarse_re = contract("kq,qrc->krc", table_re, columns)
    coarse_im = contract("kq,qrc->krc", table_im, columns)
    offsets = lax.axis_index("seq") * piece + jnp.arange(piece, dtype=jnp.int32)
    twist_re, twist_im = rotation(freq_index[:, None] * offsets[None, :], total, -1.0)
    twist_re = twist_re[:, :, None]
    twist_im = twist_im[:, :, None]
    turned_re = coarse_re * twist_re - coarse_im * twist_im
    turned_im = coarse_re * twist_im + coarse_im * twist_re
    moved = lax.all_to_all(
        jnp.stack([turned_re, turned_im]), "seq", split_axis=1, concat_axis=2, tiled=True
    )
    return local_forward(moved[0], moved[1])


def inverse_time(spec_re, spec_im, local_labels, all_labels):
    pairs, first, second, width = spec_re.shape
    rows = first * second
    steps = lax.axis_size("seq")
    double = 2 * steps
    total = double * rows
    time_re, time_im = local_inverse(spec_re, spec_im)
    positions = jnp.arange(rows, dtype=jnp.int32)
    twist_re, twist_im = rotation(local_labels[:, None] * positions[None, :], total, 1.0)
    twist_re = twist_re[:, :, None]
    twist_im = twist_im[:, :, None]
    turned_re = time_re * twist_re - time_im * twist_im
    turned_im = time_re * twist_im + time_im * twist_re
    moved = lax.all_to_all(
        jnp.stack([turned_re, turned_im]), "seq", split_axis=2, concat_axis=1, tiled=True
    )
    block_index = jnp.arange(steps, dtype=jnp.int32)
    table_re, table_im = rotation(block_index[:, None] * all_labels[None, :], double, 1.0)
    result_re = (
        contract("qk,krc->qrc", table_re, moved[0]) - contract("qk,krc->qrc", table_im, moved[1])
    ) / total
    result_im = (
        contract("qk,krc->qrc", table_re, moved[1]) + contract("qk,krc->qrc", table_im, moved[0])
    ) / total
    return (result_re, result_im)


def local(inputs, gate_values, out_grad, filter_taps, skip_gain):
    seq_input = inputs[0]
    seq_gate = gate_values[0]
    seq_grad = out_grad[0]
    rows, width = seq_input.shape
    replicas = lax.axis_size("dp")
    conv_grad = seq_grad * seq_gate
    spec_re, spec_im = forward_spectrum(
        jnp.concatenate([seq_input, conv_grad, filter_taps], axis=1)
    )
    filter_re = spec_re[..., 2 * width :]
    filter_im = spec_im[..., 2 * width :]
    input_re = spec_re[..., :width]
    input_im = spec_im[..., :width]
    grad_re = spec_re[..., width : 2 * width]
    grad_im = spec_im[..., width : 2 * width]
    conv_re = filter_re * input_re - filter_im * input_im
    conv_im = filter_re * input_im + filter_im * input_re
    corr_re = filter_re * grad_re + filter_im * grad_im
    corr_im = filter_re * grad_im - filter_im * grad_re
    taps_re = input_re * grad_re + input_im * grad_im
    taps_im = input_re * grad_im - input_im * grad_re
    packed_re = conv_re - corr_im
    packed_im = conv_im + corr_re
    local_labels, all_labels = frequency_labels()
    result_re, result_im = inverse_time(
        jnp.concatenate([packed_re, taps_re], axis=3),
        jnp.concatenate([packed_im, taps_im], axis=3),
        local_labels,
        all_labels,
    )
    results = jnp.concatenate([result_re, result_im[..., :width]], axis=2)
    timeline = lax.all_to_all(results, "seq", split_axis=0, concat_axis=1, tiled=True)[0]
    conv_time = timeline[:, :width]
    corr_time = timeline[:, timeline.shape[1] - width :]
    taps_time = timeline[:, width : timeline.shape[1] - width]
    taps_time = lax.psum_scatter(taps_time, "dp", scatter_dimension=1, tiled=True)
    gate_part = seq_grad * (conv_time + skip_gain[None, :] * seq_input)
    input_part = corr_time + skip_gain[None, :] * conv_grad
    length_total = rows * lax.axis_size("seq")
    batch_total = replicas * inputs.shape[0]
    filter_part = taps_time / math.sqrt(batch_total * length_total)
    return (input_part[None], gate_part[None], filter_part)


MESH = pl.DeviceIdType.MESH


def split_halves(table):
    high = table.astype(ml_dtypes.bfloat16)
    low = (table - high.astype(np.float64)).astype(ml_dtypes.bfloat16)
    return high, low


def block_tables(rows):
    double = 2 * rows
    place = np.arange(rows)
    turned = 2.0 * np.pi * ((place[:, None] * place[None, :]) % double) / double
    real = np.cos(turned)
    imag = -np.sin(turned)
    imag[:, 0] = 1.0 - 2.0 * (place % 2)
    forward = np.concatenate([real, imag], axis=1)
    weight = np.full((double, 1), 2.0 / double)
    weight[0] = weight[rows] = 1.0 / double
    inverse = forward.T * weight
    return split_halves(forward) + split_halves(inverse)


def dot3(values, high, low):
    top = values.astype(jnp.bfloat16)
    rest = (values - top.astype(jnp.float32)).astype(jnp.bfloat16)
    dot = functools.partial(jnp.dot, preferred_element_type=jnp.float32)
    both = dot(jnp.concatenate([top, rest], axis=0), high)
    count = values.shape[0]
    return both[:count] + (both[count:] + dot(top, low))


def kernel(
    steps, replicas, batch_total,
    in_any, gate_any, og_any, taps_any, skip_any, fh_any, fl_any, ih_any, il_any,
    ig_out, gg_out, fg_out,
    inp, gate, og, taps, skip, fh, fl, ih, il,
    sig, hsend, first_in, second_in, spec_first, spec_second, filt, prod, tprod,
    out_t, out_s, out_d, res, res_cross, res_taps, part,
    load_sem, h_send_sem, h_recv_sem, in_send_sem, in_recv_sem, out_send_sem, out_recv_sem,
    d_send_sem, d_recv_sem,
):
    devices = steps * replicas
    own_s = lax.axis_index("seq")
    own_d = lax.axis_index("dp")
    me = own_s * replicas + own_d
    rows, width = inp.shape
    lanes = 128
    half = steps // 2
    members = half * replicas
    side = own_s // half
    other = 1 - side
    place = me - members * side
    ahead = members // 2
    inner = jnp.where(side == 0, place >= ahead, place < ahead)
    cross_first = jnp.where(side == 0, 0, ahead)
    group = lax.rem(place + ahead, members)

    barrier = pltpu.get_barrier_semaphore()

    def greet(i, carry):
        p = lax.rem(me + i, devices)
        pl.semaphore_signal(
            barrier, inc=1, device_id=(p // replicas, lax.rem(p, replicas)), device_id_type=MESH
        )
        return carry

    loads = [
        pltpu.make_async_copy(src, dst, load_sem.at[k])
        for k, (src, dst) in enumerate([
            (taps_any, taps), (in_any, inp), (og_any, og), (gate_any, gate), (skip_any, skip),
            (fh_any, fh), (fl_any, fl), (ih_any, ih), (il_any, il),
        ])
    ]
    for copy in loads:
        copy.start()
    lax.fori_loop(1, devices, greet, 0)

    def remote(src, dst, src_sem, dst_sem, s, d):
        return pltpu.make_async_remote_copy(
            src_ref=src, dst_ref=dst, send_sem=src_sem, recv_sem=dst_sem,
            device_id=(s, d), device_id_type=MESH,
        )

    def arrived(ref, sem):
        pltpu.make_async_copy(ref, ref, sem).wait()

    def repeat(low, high, use):
        def body(i, carry):
            use(i)
            return carry

        lax.fori_loop(low, high, body, 0)

    def slot_of(block, of_side):
        return jnp.where(of_side == 0, steps - 1 - block, block)

    own_row = (slot_of(own_s, side) - half) * replicas + own_d
    cross_row = slot_of(own_s, other) * replicas + own_d
    h_row = lax.rem(own_s + half, steps)

    def group_at(s):
        return lax.rem(lax.rem(s, half) * replicas + own_d + ahead, members)

    h_low = jnp.where(side == 0, 0, half // 2)
    h_high = jnp.where(side == 0, steps, half + half // 2)

    def h_copy(s, sender):
        return remote(
            hsend.at[group_at(s)], first_in.at[h_row], h_send_sem.at[s], h_recv_sem.at[side], s, own_d
        )

    def h_each(use_remote, use_local):
        def body(s):
            @pl.when(s != own_s)
            def _():
                use_remote(s)

            if use_local is not None:
                @pl.when(s == own_s)
                def _():
                    use_local()

        repeat(h_low, h_high, body)

    def own_side(kind, which, dst_ref, base):
        def body(i):
            q = lax.rem(place + i, members)
            remote(
                sig.at[which, lax.rem(q + ahead, members)], dst_ref.at[base + own_row],
                in_send_sem.at[kind], in_recv_sem.at[kind],
                half * side + q // replicas, lax.rem(q, replicas),
            ).start()

        repeat(1, members, body)
        pltpu.make_async_copy(sig.at[which, group], dst_ref.at[base + own_row], in_recv_sem.at[kind]).start()

    def crossing():
        def body(i):
            q = jnp.where(side == 0, 0, ahead) + lax.rem(lax.rem(place, ahead) + i, ahead)
            remote(
                sig.at[side, lax.rem(q + ahead, members)], second_in.at[cross_row],
                in_send_sem.at[2], in_recv_sem.at[2],
                half * other + q // replicas, lax.rem(q, replicas),
            ).start()

        repeat(0, ahead, body)

    def prepare_input():
        loads[1].wait()
        sig[0] = inp[...].T.reshape(width // 8, 8, rows)

    def prepare_grad():
        loads[2].wait()
        loads[3].wait()
        gate[...] = og[...] * gate[...]
        sig[1] = gate[...].T.reshape(width // 8, 8, rows)

    loads[0].wait()
    hsend[...] = taps[...].T.reshape(width // 8, 8, rows)
    pl.when(side == 0)(prepare_input)
    pl.when(side == 1)(prepare_grad)
    pl.semaphore_wait(barrier, devices - 1)
    h_each(
        lambda s: h_copy(s, s).start(),
        lambda: pltpu.make_async_copy(hsend.at[group], first_in.at[h_row], h_recv_sem.at[side]).start(),
    )
    own_side(0, side, first_in, steps)
    crossing()
    pl.when(side == 0)(prepare_grad)
    pl.when(side == 1)(prepare_input)
    own_side(1, other, second_in, members)

    for copy in loads[4:]:
        copy.wait()

    lane = lax.broadcasted_iota(jnp.int32, (8, lanes), 1)
    sign = (1 - 2 * lax.rem(lane, 2)).astype(jnp.float32)
    turn = jnp.where(side == 0, 1.0, -1.0).astype(jnp.float32)

    def slices(c):
        re_at = pl.ds(pl.multiple_of(c * lanes, lanes), lanes)
        im_at = pl.ds(pl.multiple_of(rows + c * lanes, lanes), lanes)
        return re_at, im_at, (lane + c * lanes) == 0

    def add(total, term):
        return term if total is None else total + term

    def h_at(j):
        return (j + half) % steps

    def first_served(use):
        def body(i):
            q = lax.rem(place + i, members)
            pl.when(jnp.logical_and(q >= 4, q != place))(lambda: use(q))

        def served(q):
            pl.when(q != place)(lambda: use(q))

        repeat(0, 4, served)
        repeat(1, members, body)

    def send_own(source, base, kind, which):
        def use(q):
            s = half * side + q // replicas
            at = (slot_of(s, side) - half) * replicas + lax.rem(q, replicas)
            remote(
                source.at[base + at], res.at[which, group], out_send_sem.at[kind], out_recv_sem.at[kind],
                s, lax.rem(q, replicas),
            ).start()

        first_served(use)
        pltpu.make_async_copy(source.at[base + own_row], res.at[which, group], out_recv_sem.at[kind]).start()

    def send_cross():
        def use(q):
            s = half * other + q // replicas
            at = slot_of(s, side) * replicas + lax.rem(q, replicas)
            remote(
                out_t.at[at], res_cross.at[lax.rem(place, ahead)], out_send_sem.at[2], out_recv_sem.at[2],
                s, lax.rem(q, replicas),
            ).start()

        repeat(0, 4, use)
        repeat(0, members, lambda i: pl.when(lax.rem(place + i, members) >= 4)(lambda: use(lax.rem(place + i, members))))

    d_dst = group // (members // replicas)
    d_at = lax.rem(group, members // replicas)

    def d_each(start, use_remote, use_local):
        def body(i):
            u = start + i
            to_self = jnp.logical_and(u == own_s, d_dst == own_d)

            @pl.when(jnp.logical_not(to_self))
            def _():
                use_remote(remote(
                    out_d.at[u], res_taps.at[d_at], d_send_sem.at[u], d_recv_sem.at[0], u, d_dst
                ))

            if use_local:
                @pl.when(to_self)
                def _():
                    pltpu.make_async_copy(out_d.at[u], res_taps.at[d_at], d_recv_sem.at[0]).start()

        repeat(0, half, body)

    def part_copy():
        return remote(
            out_d.at[pl.ds(0, half)], part, d_send_sem.at[0], d_recv_sem.at[1],
            lax.rem(own_s + half, steps), own_d,
        )

    def work(low):
        count = steps - low
        def transform_first(start, size):
            spec_first[pl.ds(start, size)] = dot3(
                first_in[pl.ds(start, size)].reshape(size * 8, rows), fh[...], fl[...]
            ).reshape(size, 8, 2 * rows)

        arrived(first_in.at[pl.ds(half, half)], h_recv_sem.at[0])
        if low == 0:
            arrived(first_in.at[pl.ds(0, half)], h_recv_sem.at[1])
        transform_first(low, count)

        def prepare(c):
            re_at, im_at, first = slices(c)
            re = [spec_first[h_at(j), :, re_at] for j in range(count)]
            im = [spec_first[h_at(j), :, im_at] for j in range(count)]
            for j in range(count):
                out_re = re[j] if j == 0 else re[j] + sign * re[j - 1]
                out_im = im[j] if j == 0 else im[j] + sign * im[j - 1]
                filt[0, j, :, re_at] = out_re
                filt[1, j, :, re_at] = jnp.where(first, 0.0, turn * out_im)
                filt[2, j, :, re_at] = jnp.where(first, out_im, out_re)

        repeat(0, rows // lanes, prepare)
        arrived(first_in.at[pl.ds(steps, members)], in_recv_sem.at[0])
        transform_first(steps, members)

        def filters(re_at):
            return [[filt[i, j, :, re_at] for j in range(count)] for i in range(3)]

        def first_products(i):
            c, k = i // replicas, lax.rem(i, replicas)
            re_at, im_at, _ = slices(c)
            h_re, h_im, h_re2 = filters(re_at)
            t_re = [spec_first[steps + v * replicas + k, :, re_at] for v in range(half)]
            t_im = [spec_first[steps + v * replicas + k, :, im_at] for v in range(half)]
            for u in range(low, steps):
                re, im = None, None
                for v in range(max(u, half), steps):
                    j, w = v - u, v - half
                    re = add(re, h_re[j] * t_re[w] - h_im[j] * t_im[w])
                    im = add(im, h_re2[j] * t_im[w] + h_im[j] * t_re[w])
                prod[u * replicas + k, :, re_at] = re
                prod[u * replicas + k, :, im_at] = im

        repeat(0, rows // lanes * replicas, first_products)

        def inverse(source, start, size):
            return dot3(
                source[pl.ds(start, size)].reshape(size * 8, 2 * rows), ih[...], il[...]
            ).reshape(size, 8, rows)

        if low == 0:
            out_t[pl.ds(0, members)] = inverse(prod, 0, members)
            send_cross()
        out_t[pl.ds(members, members)] = inverse(prod, members, members)
        send_own(out_t, members, 0, side)

        def transform(start):
            spec_second[pl.ds(start, members)] = dot3(
                second_in[pl.ds(start, members)].reshape(members * 8, rows), fh[...], fl[...]
            ).reshape(members, 8, 2 * rows)

        def second_products(begin, end, extend):
            def body(i):
                c, k = i // replicas, lax.rem(i, replicas)
                re_at, im_at, _ = slices(c)
                h_re, h_im, h_re2 = filters(re_at)
                s_re = [spec_second[v * replicas + k, :, re_at] for v in range(begin, end)]
                s_im = [spec_second[v * replicas + k, :, im_at] for v in range(begin, end)]
                for u in range(half, steps):
                    at = (u - half) * replicas + k
                    re, im = (prod[at, :, re_at], prod[at, :, im_at]) if extend else (None, None)
                    for v in range(begin, min(u + 1, end)):
                        j, w = u - v, v - begin
                        re = add(re, h_re[j] * s_re[w] + h_im[j] * s_im[w])
                        im = add(im, h_re2[j] * s_im[w] - h_im[j] * s_re[w])
                    prod[at, :, re_at] = re
                    prod[at, :, im_at] = im

            repeat(0, rows // lanes * replicas, body)

        def taps_products(begin, end, extend):
            def body(c):
                re_at, im_at, first = slices(c)
                flip = jnp.where(first, 1.0, -turn)
                sums_re, sums_im = [None] * (steps + 1), [None] * (steps + 1)
                for k in range(replicas):
                    t_re = [spec_first[steps + v * replicas + k, :, re_at] for v in range(half)]
                    t_im = [spec_first[steps + v * replicas + k, :, im_at] for v in range(half)]
                    for s in range(begin, end):
                        s_re = spec_second[s * replicas + k, :, re_at]
                        s_im = spec_second[s * replicas + k, :, im_at]
                        s_re2 = jnp.where(first, s_im, s_re)
                        s_im = jnp.where(first, 0.0, s_im)
                        for v in range(max(s, half), steps):
                            m, w = v - s, v - half
                            sums_re[m] = add(sums_re[m], t_re[w] * s_re + t_im[w] * s_im)
                            sums_im[m] = add(sums_im[m], t_im[w] * s_re2 - t_re[w] * s_im)

                def folded(sums, m):
                    if sums[m] is None:
                        return sign * sums[m + 1]
                    return sums[m] if sums[m + 1] is None else sums[m] + sign * sums[m + 1]

                for m in range(half if end == steps else steps):
                    re, im = folded(sums_re, m), flip * folded(sums_im, m)
                    tprod[m, :, re_at] = tprod[m, :, re_at] + re if extend else re
                    tprod[m, :, im_at] = tprod[m, :, im_at] + im if extend else im

            repeat(0, rows // lanes, body)

        def finish_second():
            second_products(half, steps, low == 0)
            out_s[...] = inverse(prod, 0, members)
            send_own(out_s, 0, 1, other)

        def finish_taps():
            taps_products(half, steps, low == 0)
            out_d[pl.ds(0, half)] = inverse(tprod, 0, half)
            if low == 0:
                arrived(part, d_recv_sem.at[1])
                out_d[pl.ds(0, half)] = out_d[pl.ds(0, half)] + part[...]
                d_each(0, lambda copy: copy.start(), True)
            else:
                part_copy().start()

        if low == 0:
            arrived(second_in.at[pl.ds(0, members)], in_recv_sem.at[2])
            transform(0)
            taps_products(0, half, False)
            out_d[pl.ds(half, half)] = inverse(tprod, half, half)
            d_each(half, lambda copy: copy.start(), True)
            second_products(0, half, False)
        arrived(second_in.at[pl.ds(members, members)], in_recv_sem.at[1])
        transform(members)
        if low == 0:
            finish_taps()
            finish_second()
        else:
            finish_taps()
            finish_second()

    pl.when(inner)(lambda: work(0))
    pl.when(jnp.logical_not(inner))(lambda: work(half))

    gain = skip[...]

    def positions(which):
        return res[which].reshape(width, rows).T

    def finish(is_second):
        ranges = pl.ds(0, ahead) if is_second else pl.ds(ahead, ahead)
        arrived(res.at[1 if is_second else 0], out_recv_sem.at[0])
        if is_second:
            ig_out[...] = positions(1) + gain * gate[...]
        else:
            gg_out[...] = og[...] * (positions(0) + gain * inp[...])
        late = 0 if is_second else 1
        arrived(res_cross, out_recv_sem.at[2])
        arrived(res.at[late], out_recv_sem.at[1])
        res[late, ranges] = res[late, ranges] + res_cross[...]
        if is_second:
            gg_out[...] = og[...] * (positions(0) + gain * inp[...])
        else:
            ig_out[...] = positions(1) + gain * gate[...]
        scale = 1.0 / math.sqrt(batch_total * rows * steps)
        arrived(res_taps, d_recv_sem.at[0])
        fg_out[...] = scale * res_taps[...].reshape(width // replicas, rows)

    pl.when(side == 0)(lambda: finish(False))
    pl.when(side == 1)(lambda: finish(True))

    h_each(lambda s: h_copy(s, s).wait_send(), None)
    arrived(sig.at[0, pl.ds(0, members - 1)], in_send_sem.at[0])
    arrived(sig.at[0, pl.ds(0, members - 1)], in_send_sem.at[1])
    arrived(sig.at[0, pl.ds(0, ahead)], in_send_sem.at[2])
    arrived(sig.at[0, pl.ds(0, members - 1)], out_send_sem.at[0])
    arrived(sig.at[0, pl.ds(0, members - 1)], out_send_sem.at[1])

    @pl.when(inner)
    def _():
        arrived(sig.at[0], out_send_sem.at[2])
        d_each(0, lambda copy: copy.wait_send(), False)
        d_each(half, lambda copy: copy.wait_send(), False)

    @pl.when(jnp.logical_not(inner))
    def _():
        part_copy().wait_send()


def hand_over(*refs):
    writes = [pltpu.make_async_copy(refs[k], refs[3 + k], refs[6].at[k]) for k in range(3)]
    for copy in writes:
        copy.start()
    for copy in writes:
        copy.wait()


def fused(inputs, gate_values, out_grad, filter_taps, skip_gain, steps, replicas):
    rows, width = filter_taps.shape
    double = 2 * rows
    members = steps * replicas // 2
    tables = block_tables(rows)
    f32, bf16 = jnp.float32, jnp.bfloat16
    dma = pltpu.SemaphoreType.DMA
    anywhere = pl.BlockSpec(memory_space=pltpu.HBM)
    near = pl.BlockSpec(memory_space=pltpu.VMEM)
    block = pltpu.VMEM((rows, width), f32)

    def tiles(*shape):
        return pltpu.VMEM(shape + (8, rows), f32)

    def spectra(count):
        return pltpu.VMEM((count, 8, double), f32)

    results = pl.pallas_call(
        functools.partial(kernel, steps, replicas, replicas * inputs.shape[0]),
        out_shape=(
            pltpu.VMEM((rows, width), f32),
            pltpu.VMEM((rows, width), f32),
            pltpu.VMEM((width // replicas, rows), f32),
        ),
        in_specs=[anywhere] * 9,
        out_specs=(near, near, near),
        scratch_shapes=[block, block, block, block, pltpu.VMEM((1, width), f32)]
        + [pltpu.VMEM((rows, double), bf16)] * 2
        + [pltpu.VMEM((double, rows), bf16)] * 2
        + [tiles(2, width // 8), tiles(width // 8), tiles(steps + members), tiles(2 * members)]
        + [spectra(steps + members), spectra(2 * members), tiles(3, steps)]
        + [spectra(2 * members), spectra(steps)]
        + [tiles(2 * members), tiles(members), tiles(steps)]
        + [tiles(2, width // 8), tiles(width // 16), tiles(width // 8 // replicas), tiles(steps // 2)]
        + [dma((9,)), dma((steps,)), dma((2,)), dma((3,)), dma((3,)), dma((3,)), dma((3,)), dma((steps,)), dma((2,))],
        compiler_params=pltpu.CompilerParams(
            collective_id=0, has_side_effects=True, vmem_limit_bytes=48 * 1024 * 1024
        ),
    )(
        *[
            pltpu.with_memory_space_constraint(value, pltpu.HBM)
            for value in (
                inputs[0], gate_values[0], out_grad[0], filter_taps, skip_gain[None, :],
                *[jnp.asarray(table) for table in tables],
            )
        ],
    )
    input_part, gate_part, filter_part = pl.pallas_call(
        hand_over,
        out_shape=tuple(jax.ShapeDtypeStruct(part.shape, part.dtype) for part in results),
        in_specs=[near] * 3,
        out_specs=(anywhere,) * 3,
        scratch_shapes=[dma((3,))],
        compiler_params=pltpu.CompilerParams(vmem_limit_bytes=2 * 1024 * 1024),
    )(*results)
    return input_part[None], gate_part[None], filter_part.T


def solution(mesh):
    placed = (P("dp", "seq", None), P("dp", "seq", None), P("dp", "seq", None), P("seq", None), P())
    steps, replicas = mesh.shape["seq"], mesh.shape["dp"]

    def either(inputs, gate_values, out_grad, filter_taps, skip_gain):
        rows, width = filter_taps.shape
        fits = width == 128 and (steps, replicas) == (8, 4) and rows % 128 == 0
        if fits and inputs.shape[0] == 1:
            return fused(inputs, gate_values, out_grad, filter_taps, skip_gain, steps, replicas)
        return local(inputs, gate_values, out_grad, filter_taps, skip_gain)

    return jax.shard_map(
        either,
        mesh=mesh,
        in_specs=placed,
        out_specs=(P("dp", "seq", None), P("dp", "seq", None), P("seq", "dp")),
        check_vma=False,
    )
```

```python
import functools
import math

import jax
import jax.numpy as jnp
import ml_dtypes
import numpy as np
from jax import lax
from jax.experimental import pallas as pl
from jax.experimental.pallas import tpu as pltpu
from jax.sharding import PartitionSpec as P

first_radix = 32


def rotation(product, modulus, direction):
    fraction = (product % modulus).astype(jnp.float32) / modulus
    turned = 2.0 * math.pi * fraction
    return (jnp.cos(turned), direction * jnp.sin(turned))


def contract(formula, matrix, operand):
    return jnp.einsum(
        formula,
        matrix,
        operand,
        precision=lax.Precision.HIGHEST,
        preferred_element_type=jnp.float32,
    )


def complex_apply(formula, table_re, table_im, values_re, values_im):
    result_re = contract(formula, table_re, values_re) - contract(formula, table_im, values_im)
    result_im = contract(formula, table_re, values_im) + contract(formula, table_im, values_re)
    return (result_re, result_im)


def local_forward(values_re, values_im):
    pairs, rows, width = values_re.shape
    second = rows // first_radix
    values_re = values_re.reshape(pairs, first_radix, second, width)
    values_im = values_im.reshape(pairs, first_radix, second, width)
    outer = jnp.arange(first_radix, dtype=jnp.int32)
    inner = jnp.arange(second, dtype=jnp.int32)
    table_re, table_im = rotation(outer[:, None] * outer[None, :], first_radix, -1.0)
    section_re, section_im = complex_apply(
        "ca,mabx->mcbx", table_re, table_im, values_re, values_im
    )
    twist_re, twist_im = rotation(outer[:, None] * inner[None, :], rows, -1.0)
    twist_re = twist_re[None, :, :, None]
    twist_im = twist_im[None, :, :, None]
    turned_re = section_re * twist_re - section_im * twist_im
    turned_im = section_re * twist_im + section_im * twist_re
    table_re, table_im = rotation(inner[:, None] * inner[None, :], second, -1.0)
    return complex_apply("db,mcbx->mcdx", table_re, table_im, turned_re, turned_im)


def local_inverse(spec_re, spec_im):
    pairs, first, second, width = spec_re.shape
    rows = first * second
    outer = jnp.arange(first, dtype=jnp.int32)
    inner = jnp.arange(second, dtype=jnp.int32)
    table_re, table_im = rotation(inner[:, None] * inner[None, :], second, 1.0)
    section_re, section_im = complex_apply("bd,mcdx->mcbx", table_re, table_im, spec_re, spec_im)
    twist_re, twist_im = rotation(outer[:, None] * inner[None, :], rows, 1.0)
    twist_re = twist_re[None, :, :, None]
    twist_im = twist_im[None, :, :, None]
    turned_re = section_re * twist_re - section_im * twist_im
    turned_im = section_re * twist_im + section_im * twist_re
    table_re, table_im = rotation(outer[:, None] * outer[None, :], first, 1.0)
    result_re, result_im = complex_apply("ac,mcbx->mabx", table_re, table_im, turned_re, turned_im)
    return (result_re.reshape(pairs, rows, width), result_im.reshape(pairs, rows, width))


def frequency_labels():
    steps = lax.axis_size("seq")
    own = lax.axis_index("seq")
    local_labels = 2 * own + jnp.arange(2, dtype=jnp.int32)
    all_labels = jnp.arange(2 * steps, dtype=jnp.int32)
    return (local_labels, all_labels)


def forward_spectrum(signal):
    rows, width = signal.shape
    steps = lax.axis_size("seq")
    piece = rows // steps
    double = 2 * steps
    total = double * rows
    columns = lax.all_to_all(
        signal.reshape(1, rows, width), "seq", split_axis=1, concat_axis=0, tiled=True
    )
    block_index = jnp.arange(steps, dtype=jnp.int32)
    freq_index = jnp.arange(double, dtype=jnp.int32)
    table_re, table_im = rotation(freq_index[:, None] * block_index[None, :], double, -1.0)
    coarse_re = contract("kq,qrc->krc", table_re, columns)
    coarse_im = contract("kq,qrc->krc", table_im, columns)
    offsets = lax.axis_index("seq") * piece + jnp.arange(piece, dtype=jnp.int32)
    twist_re, twist_im = rotation(freq_index[:, None] * offsets[None, :], total, -1.0)
    twist_re = twist_re[:, :, None]
    twist_im = twist_im[:, :, None]
    turned_re = coarse_re * twist_re - coarse_im * twist_im
    turned_im = coarse_re * twist_im + coarse_im * twist_re
    moved = lax.all_to_all(
        jnp.stack([turned_re, turned_im]), "seq", split_axis=1, concat_axis=2, tiled=True
    )
    return local_forward(moved[0], moved[1])


def inverse_time(spec_re, spec_im, local_labels, all_labels):
    pairs, first, second, width = spec_re.shape
    rows = first * second
    steps = lax.axis_size("seq")
    double = 2 * steps
    total = double * rows
    time_re, time_im = local_inverse(spec_re, spec_im)
    positions = jnp.arange(rows, dtype=jnp.int32)
    twist_re, twist_im = rotation(local_labels[:, None] * positions[None, :], total, 1.0)
    twist_re = twist_re[:, :, None]
    twist_im = twist_im[:, :, None]
    turned_re = time_re * twist_re - time_im * twist_im
    turned_im = time_re * twist_im + time_im * twist_re
    moved = lax.all_to_all(
        jnp.stack([turned_re, turned_im]), "seq", split_axis=2, concat_axis=1, tiled=True
    )
    block_index = jnp.arange(steps, dtype=jnp.int32)
    table_re, table_im = rotation(block_index[:, None] * all_labels[None, :], double, 1.0)
    result_re = (
        contract("qk,krc->qrc", table_re, moved[0]) - contract("qk,krc->qrc", table_im, moved[1])
    ) / total
    result_im = (
        contract("qk,krc->qrc", table_re, moved[1]) + contract("qk,krc->qrc", table_im, moved[0])
    ) / total
    return (result_re, result_im)


def local(inputs, gate_values, out_grad, filter_taps, skip_gain):
    seq_input = inputs[0]
    seq_gate = gate_values[0]
    seq_grad = out_grad[0]
    rows, width = seq_input.shape
    replicas = lax.axis_size("dp")
    conv_grad = seq_grad * seq_gate
    spec_re, spec_im = forward_spectrum(
        jnp.concatenate([seq_input, conv_grad, filter_taps], axis=1)
    )
    filter_re = spec_re[..., 2 * width :]
    filter_im = spec_im[..., 2 * width :]
    input_re = spec_re[..., :width]
    input_im = spec_im[..., :width]
    grad_re = spec_re[..., width : 2 * width]
    grad_im = spec_im[..., width : 2 * width]
    conv_re = filter_re * input_re - filter_im * input_im
    conv_im = filter_re * input_im + filter_im * input_re
    corr_re = filter_re * grad_re + filter_im * grad_im
    corr_im = filter_re * grad_im - filter_im * grad_re
    taps_re = input_re * grad_re + input_im * grad_im
    taps_im = input_re * grad_im - input_im * grad_re
    packed_re = conv_re - corr_im
    packed_im = conv_im + corr_re
    local_labels, all_labels = frequency_labels()
    result_re, result_im = inverse_time(
        jnp.concatenate([packed_re, taps_re], axis=3),
        jnp.concatenate([packed_im, taps_im], axis=3),
        local_labels,
        all_labels,
    )
    results = jnp.concatenate([result_re, result_im[..., :width]], axis=2)
    timeline = lax.all_to_all(results, "seq", split_axis=0, concat_axis=1, tiled=True)[0]
    conv_time = timeline[:, :width]
    corr_time = timeline[:, timeline.shape[1] - width :]
    taps_time = timeline[:, width : timeline.shape[1] - width]
    taps_time = lax.psum_scatter(taps_time, "dp", scatter_dimension=1, tiled=True)
    gate_part = seq_grad * (conv_time + skip_gain[None, :] * seq_input)
    input_part = corr_time + skip_gain[None, :] * conv_grad
    length_total = rows * lax.axis_size("seq")
    batch_total = replicas * inputs.shape[0]
    filter_part = taps_time / math.sqrt(batch_total * length_total)
    return (input_part[None], gate_part[None], filter_part)


MESH = pl.DeviceIdType.MESH


def split_halves(table):
    high = table.astype(ml_dtypes.bfloat16)
    low = (table - high.astype(np.float64)).astype(ml_dtypes.bfloat16)
    return high, low


def block_tables(rows):
    double = 2 * rows
    place = np.arange(rows)
    turned = 2.0 * np.pi * ((place[:, None] * place[None, :]) % double) / double
    real = np.cos(turned)
    imag = -np.sin(turned)
    imag[:, 0] = 1.0 - 2.0 * (place % 2)
    forward = np.concatenate([real, imag], axis=1)
    weight = np.full((double, 1), 2.0 / double)
    weight[0] = weight[rows] = 1.0 / double
    inverse = forward.T * weight
    return split_halves(forward) + split_halves(inverse)


def dot3(values, high, low):
    top = values.astype(jnp.bfloat16)
    rest = (values - top.astype(jnp.float32)).astype(jnp.bfloat16)
    dot = functools.partial(jnp.dot, preferred_element_type=jnp.float32)
    both = dot(jnp.concatenate([top, rest], axis=0), high)
    count = values.shape[0]
    return both[:count] + (both[count:] + dot(top, low))


def kernel(
    steps, replicas, batch_total,
    in_any, gate_any, og_any, taps_any, skip_any, fh_any, fl_any, ih_any, il_any,
    ig_out, gg_out, fg_out,
    inp, gate, og, taps, skip, fh, fl, ih, il,
    sig, hsend, first_in, second_in, spec_first, spec_second, filt, prod, tprod,
    out_t, out_s, out_d, res, res_cross, res_taps, part,
    load_sem, h_send_sem, h_recv_sem, in_send_sem, in_recv_sem, out_send_sem, out_recv_sem,
    d_send_sem, d_recv_sem,
):
    devices = steps * replicas
    own_s = lax.axis_index("seq")
    own_d = lax.axis_index("dp")
    me = own_s * replicas + own_d
    rows, width = inp.shape
    lanes = 128
    half = steps // 2
    members = half * replicas
    side = own_s // half
    other = 1 - side
    place = me - members * side
    ahead = members // 2
    inner = jnp.where(side == 0, place >= ahead, place < ahead)
    cross_first = jnp.where(side == 0, 0, ahead)
    group = lax.rem(place + ahead, members)

    barrier = pltpu.get_barrier_semaphore()

    def greet(i, carry):
        p = lax.rem(me + i, devices)
        pl.semaphore_signal(
            barrier, inc=1, device_id=(p // replicas, lax.rem(p, replicas)), device_id_type=MESH
        )
        return carry

    loads = [
        pltpu.make_async_copy(src, dst, load_sem.at[k])
        for k, (src, dst) in enumerate([
            (taps_any, taps), (in_any, inp), (og_any, og), (gate_any, gate), (skip_any, skip),
            (fh_any, fh), (fl_any, fl), (ih_any, ih), (il_any, il),
        ])
    ]
    for copy in loads:
        copy.start()
    lax.fori_loop(1, devices, greet, 0)

    def remote(src, dst, src_sem, dst_sem, s, d):
        return pltpu.make_async_remote_copy(
            src_ref=src, dst_ref=dst, send_sem=src_sem, recv_sem=dst_sem,
            device_id=(s, d), device_id_type=MESH,
        )

    def arrived(ref, sem):
        pltpu.make_async_copy(ref, ref, sem).wait()

    def repeat(low, high, use, unroll=1):
        def body(i, carry):
            use(i)
            return carry

        lax.fori_loop(low, high, body, 0, unroll=unroll)

    def slot_of(block, of_side):
        return jnp.where(of_side == 0, steps - 1 - block, block)

    own_row = (slot_of(own_s, side) - half) * replicas + own_d
    cross_row = slot_of(own_s, other) * replicas + own_d
    h_row = lax.rem(own_s + half, steps)

    def group_at(s):
        return lax.rem(lax.rem(s, half) * replicas + own_d + ahead, members)

    h_low = jnp.where(side == 0, 0, half // 2)
    h_high = jnp.where(side == 0, steps, half + half // 2)

    def h_copy(s, sender):
        return remote(
            hsend.at[group_at(s)], first_in.at[h_row], h_send_sem.at[s], h_recv_sem.at[side], s, own_d
        )

    def h_each(use_remote, use_local):
        def body(s):
            @pl.when(s != own_s)
            def _():
                use_remote(s)

            if use_local is not None:
                @pl.when(s == own_s)
                def _():
                    use_local()

        repeat(h_low, h_high, body)

    def own_side(kind, which, dst_ref, base):
        def body(i):
            q = lax.rem(place + i, members)
            remote(
                sig.at[which, lax.rem(q + ahead, members)], dst_ref.at[base + own_row],
                in_send_sem.at[kind], in_recv_sem.at[kind],
                half * side + q // replicas, lax.rem(q, replicas),
            ).start()

        repeat(1, members, body)
        pltpu.make_async_copy(sig.at[which, group], dst_ref.at[base + own_row], in_recv_sem.at[kind]).start()

    def crossing():
        def body(i):
            q = jnp.where(side == 0, 0, ahead) + lax.rem(lax.rem(place, ahead) + i, ahead)
            remote(
                sig.at[side, lax.rem(q + ahead, members)], second_in.at[cross_row],
                in_send_sem.at[2], in_recv_sem.at[2],
                half * other + q // replicas, lax.rem(q, replicas),
            ).start()

        repeat(0, ahead, body)

    def prepare_input():
        loads[1].wait()
        sig[0] = inp[...].T.reshape(width // 8, 8, rows)

    def prepare_grad():
        loads[2].wait()
        loads[3].wait()
        gate[...] = og[...] * gate[...]
        sig[1] = gate[...].T.reshape(width // 8, 8, rows)

    loads[0].wait()
    hsend[...] = taps[...].T.reshape(width // 8, 8, rows)
    pl.when(side == 0)(prepare_input)
    pl.when(side == 1)(prepare_grad)
    pl.semaphore_wait(barrier, devices - 1)
    h_each(
        lambda s: h_copy(s, s).start(),
        lambda: pltpu.make_async_copy(hsend.at[group], first_in.at[h_row], h_recv_sem.at[side]).start(),
    )
    own_side(0, side, first_in, steps)
    crossing()
    pl.when(side == 0)(prepare_grad)
    pl.when(side == 1)(prepare_input)
    own_side(1, other, second_in, members)

    for copy in loads[4:]:
        copy.wait()

    lane = lax.broadcasted_iota(jnp.int32, (8, lanes), 1)
    sign = (1 - 2 * lax.rem(lane, 2)).astype(jnp.float32)
    turn = jnp.where(side == 0, 1.0, -1.0).astype(jnp.float32)

    def slices(c):
        re_at = pl.ds(pl.multiple_of(c * lanes, lanes), lanes)
        im_at = pl.ds(pl.multiple_of(rows + c * lanes, lanes), lanes)
        return re_at, im_at, (lane + c * lanes) == 0

    def add(total, term):
        return term if total is None else total + term

    def h_at(j):
        return (j + half) % steps

    def first_served(use):
        def body(i):
            q = lax.rem(place + i, members)
            pl.when(jnp.logical_and(q >= 4, q != place))(lambda: use(q))

        def served(q):
            pl.when(q != place)(lambda: use(q))

        repeat(0, 4, served)
        repeat(1, members, body)

    def send_own(source, base, kind, which):
        def use(q):
            s = half * side + q // replicas
            at = (slot_of(s, side) - half) * replicas + lax.rem(q, replicas)
            remote(
                source.at[base + at], res.at[which, group], out_send_sem.at[kind], out_recv_sem.at[kind],
                s, lax.rem(q, replicas),
            ).start()

        first_served(use)
        pltpu.make_async_copy(source.at[base + own_row], res.at[which, group], out_recv_sem.at[kind]).start()

    def send_cross():
        def use(q):
            s = half * other + q // replicas
            at = slot_of(s, side) * replicas + lax.rem(q, replicas)
            remote(
                out_t.at[at], res_cross.at[lax.rem(place, ahead)], out_send_sem.at[2], out_recv_sem.at[2],
                s, lax.rem(q, replicas),
            ).start()

        repeat(0, 4, use)
        repeat(0, members, lambda i: pl.when(lax.rem(place + i, members) >= 4)(lambda: use(lax.rem(place + i, members))))

    d_dst = group // (members // replicas)
    d_at = lax.rem(group, members // replicas)

    def d_each(start, use_remote, use_local):
        def body(i):
            u = start + i
            to_self = jnp.logical_and(u == own_s, d_dst == own_d)

            @pl.when(jnp.logical_not(to_self))
            def _():
                use_remote(remote(
                    out_d.at[u], res_taps.at[d_at], d_send_sem.at[u], d_recv_sem.at[0], u, d_dst
                ))

            if use_local:
                @pl.when(to_self)
                def _():
                    pltpu.make_async_copy(out_d.at[u], res_taps.at[d_at], d_recv_sem.at[0]).start()

        repeat(0, half, body)

    def part_copy():
        return remote(
            out_d.at[pl.ds(0, half)], part, d_send_sem.at[0], d_recv_sem.at[1],
            lax.rem(own_s + half, steps), own_d,
        )

    def work(low):
        count = steps - low
        def transform_first(start, size):
            spec_first[pl.ds(start, size)] = dot3(
                first_in[pl.ds(start, size)].reshape(size * 8, rows), fh[...], fl[...]
            ).reshape(size, 8, 2 * rows)

        arrived(first_in.at[pl.ds(half, half)], h_recv_sem.at[0])
        if low == 0:
            arrived(first_in.at[pl.ds(0, half)], h_recv_sem.at[1])
        transform_first(low, count)

        def prepare(c):
            re_at, im_at, first = slices(c)
            re = [spec_first[h_at(j), :, re_at] for j in range(count)]
            im = [spec_first[h_at(j), :, im_at] for j in range(count)]
            for j in range(count):
                out_re = re[j] if j == 0 else re[j] + sign * re[j - 1]
                out_im = im[j] if j == 0 else im[j] + sign * im[j - 1]
                filt[0, j, :, re_at] = out_re
                filt[1, j, :, re_at] = jnp.where(first, 0.0, turn * out_im)
                filt[2, j, :, re_at] = jnp.where(first, out_im, out_re)

        repeat(0, rows // lanes, prepare)
        arrived(first_in.at[pl.ds(steps, members)], in_recv_sem.at[0])
        transform_first(steps, members)

        def filters(re_at):
            return [[filt[i, j, :, re_at] for j in range(count)] for i in range(3)]

        def first_products(i):
            c, k = i // replicas, lax.rem(i, replicas)
            re_at, im_at, _ = slices(c)
            h_re, h_im, h_re2 = filters(re_at)
            t_re = [spec_first[steps + v * replicas + k, :, re_at] for v in range(half)]
            t_im = [spec_first[steps + v * replicas + k, :, im_at] for v in range(half)]
            for u in range(low, steps):
                re, im = None, None
                for v in range(max(u, half), steps):
                    j, w = v - u, v - half
                    re = add(re, h_re[j] * t_re[w] - h_im[j] * t_im[w])
                    im = add(im, h_re2[j] * t_im[w] + h_im[j] * t_re[w])
                prod[u * replicas + k, :, re_at] = re
                prod[u * replicas + k, :, im_at] = im

        repeat(0, rows // lanes * replicas, first_products, 4)

        def inverse(source, start, size):
            return dot3(
                source[pl.ds(start, size)].reshape(size * 8, 2 * rows), ih[...], il[...]
            ).reshape(size, 8, rows)

        if low == 0:
            out_t[...] = inverse(prod, 0, 2 * members)
            send_cross()
        else:
            out_t[pl.ds(members, members)] = inverse(prod, members, members)
        send_own(out_t, members, 0, side)

        def transform(start):
            spec_second[pl.ds(start, members)] = dot3(
                second_in[pl.ds(start, members)].reshape(members * 8, rows), fh[...], fl[...]
            ).reshape(members, 8, 2 * rows)

        def second_products(begin, end, extend):
            def body(i):
                c, k = i // replicas, lax.rem(i, replicas)
                re_at, im_at, _ = slices(c)
                h_re, h_im, h_re2 = filters(re_at)
                s_re = [spec_second[v * replicas + k, :, re_at] for v in range(begin, end)]
                s_im = [spec_second[v * replicas + k, :, im_at] for v in range(begin, end)]
                for u in range(half, steps):
                    at = (u - half) * replicas + k
                    re, im = (prod[at, :, re_at], prod[at, :, im_at]) if extend else (None, None)
                    for v in range(begin, min(u + 1, end)):
                        j, w = u - v, v - begin
                        re = add(re, h_re[j] * s_re[w] + h_im[j] * s_im[w])
                        im = add(im, h_re2[j] * s_im[w] - h_im[j] * s_re[w])
                    prod[at, :, re_at] = re
                    prod[at, :, im_at] = im

            repeat(0, rows // lanes * replicas, body, 4)

        def taps_products(begin, end, extend):
            def body(c):
                re_at, im_at, first = slices(c)
                flip = jnp.where(first, 1.0, -turn)
                sums_re, sums_im = [None] * (steps + 1), [None] * (steps + 1)
                for k in range(replicas):
                    t_re = [spec_first[steps + v * replicas + k, :, re_at] for v in range(half)]
                    t_im = [spec_first[steps + v * replicas + k, :, im_at] for v in range(half)]
                    for s in range(begin, end):
                        s_re = spec_second[s * replicas + k, :, re_at]
                        s_im = spec_second[s * replicas + k, :, im_at]
                        s_re2 = jnp.where(first, s_im, s_re)
                        s_im = jnp.where(first, 0.0, s_im)
                        for v in range(max(s, half), steps):
                            m, w = v - s, v - half
                            sums_re[m] = add(sums_re[m], t_re[w] * s_re + t_im[w] * s_im)
                            sums_im[m] = add(sums_im[m], t_im[w] * s_re2 - t_re[w] * s_im)

                def folded(sums, m):
                    if sums[m] is None:
                        return sign * sums[m + 1]
                    return sums[m] if sums[m + 1] is None else sums[m] + sign * sums[m + 1]

                for m in range(half if end == steps else steps):
                    re, im = folded(sums_re, m), flip * folded(sums_im, m)
                    tprod[m, :, re_at] = tprod[m, :, re_at] + re if extend else re
                    tprod[m, :, im_at] = tprod[m, :, im_at] + im if extend else im

            repeat(0, rows // lanes, body)

        def finish_second():
            second_products(half, steps, low == 0)
            out_s[...] = inverse(prod, 0, members)
            send_own(out_s, 0, 1, other)

        def finish_taps():
            taps_products(half, steps, low == 0)
            out_d[pl.ds(0, half)] = inverse(tprod, 0, half)
            if low == 0:
                arrived(part, d_recv_sem.at[1])
                out_d[pl.ds(0, half)] = out_d[pl.ds(0, half)] + part[...]
                d_each(0, lambda copy: copy.start(), True)
            else:
                part_copy().start()

        if low == 0:
            arrived(second_in.at[pl.ds(0, members)], in_recv_sem.at[2])
            transform(0)
            taps_products(0, half, False)
            out_d[pl.ds(half, half)] = inverse(tprod, half, half)
            d_each(half, lambda copy: copy.start(), True)
            second_products(0, half, False)
        arrived(second_in.at[pl.ds(members, members)], in_recv_sem.at[1])
        transform(members)
        if low == 0:
            finish_taps()
            finish_second()
        else:
            finish_taps()
            finish_second()

    pl.when(inner)(lambda: work(0))
    pl.when(jnp.logical_not(inner))(lambda: work(half))

    gain = skip[...]

    def positions(which):
        return res[which].reshape(width, rows).T

    def finish(is_second):
        ranges = pl.ds(0, ahead) if is_second else pl.ds(ahead, ahead)
        arrived(res.at[1 if is_second else 0], out_recv_sem.at[0])
        if is_second:
            ig_out[...] = positions(1) + gain * gate[...]
        else:
            gg_out[...] = og[...] * (positions(0) + gain * inp[...])
        late = 0 if is_second else 1
        scale = 1.0 / math.sqrt(batch_total * rows * steps)
        arrived(res_taps, d_recv_sem.at[0])
        fg_out[...] = scale * res_taps[...].reshape(width // replicas, rows)
        arrived(res_cross, out_recv_sem.at[2])
        arrived(res.at[late], out_recv_sem.at[1])
        res[late, ranges] = res[late, ranges] + res_cross[...]
        if is_second:
            gg_out[...] = og[...] * (positions(0) + gain * inp[...])
        else:
            ig_out[...] = positions(1) + gain * gate[...]

    h_each(lambda s: h_copy(s, s).wait_send(), None)
    arrived(sig.at[0, pl.ds(0, members - 1)], in_send_sem.at[0])
    arrived(sig.at[0, pl.ds(0, members - 1)], in_send_sem.at[1])
    arrived(sig.at[0, pl.ds(0, ahead)], in_send_sem.at[2])

    @pl.when(inner)
    def _():
        d_each(half, lambda copy: copy.wait_send(), False)

    pl.when(side == 0)(lambda: finish(False))
    pl.when(side == 1)(lambda: finish(True))

    arrived(sig.at[0, pl.ds(0, members - 1)], out_send_sem.at[0])
    arrived(sig.at[0, pl.ds(0, members - 1)], out_send_sem.at[1])

    @pl.when(inner)
    def _():
        arrived(sig.at[0], out_send_sem.at[2])
        d_each(0, lambda copy: copy.wait_send(), False)

    @pl.when(jnp.logical_not(inner))
    def _():
        part_copy().wait_send()


def hand_over(*refs):
    writes = [pltpu.make_async_copy(refs[k], refs[3 + k], refs[6].at[k]) for k in range(3)]
    for copy in writes:
        copy.start()
    for copy in writes:
        copy.wait()


def fused(inputs, gate_values, out_grad, filter_taps, skip_gain, steps, replicas):
    rows, width = filter_taps.shape
    double = 2 * rows
    members = steps * replicas // 2
    tables = block_tables(rows)
    f32, bf16 = jnp.float32, jnp.bfloat16
    dma = pltpu.SemaphoreType.DMA
    anywhere = pl.BlockSpec(memory_space=pltpu.HBM)
    near = pl.BlockSpec(memory_space=pltpu.VMEM)
    block = pltpu.VMEM((rows, width), f32)

    def tiles(*shape):
        return pltpu.VMEM(shape + (8, rows), f32)

    def spectra(count):
        return pltpu.VMEM((count, 8, double), f32)

    results = pl.pallas_call(
        functools.partial(kernel, steps, replicas, replicas * inputs.shape[0]),
        out_shape=(
            pltpu.VMEM((rows, width), f32),
            pltpu.VMEM((rows, width), f32),
            pltpu.VMEM((width // replicas, rows), f32),
        ),
        in_specs=[anywhere] * 9,
        out_specs=(near, near, near),
        scratch_shapes=[block, block, block, block, pltpu.VMEM((1, width), f32)]
        + [pltpu.VMEM((rows, double), bf16)] * 2
        + [pltpu.VMEM((double, rows), bf16)] * 2
        + [tiles(2, width // 8), tiles(width // 8), tiles(steps + members), tiles(2 * members)]
        + [spectra(steps + members), spectra(2 * members), tiles(3, steps)]
        + [spectra(2 * members), spectra(steps)]
        + [tiles(2 * members), tiles(members), tiles(steps)]
        + [tiles(2, width // 8), tiles(width // 16), tiles(width // 8 // replicas), tiles(steps // 2)]
        + [dma((9,)), dma((steps,)), dma((2,)), dma((3,)), dma((3,)), dma((3,)), dma((3,)), dma((steps,)), dma((2,))],
        compiler_params=pltpu.CompilerParams(
            collective_id=0, has_side_effects=True, vmem_limit_bytes=48 * 1024 * 1024
        ),
    )(
        *[
            pltpu.with_memory_space_constraint(value, pltpu.HBM)
            for value in (
                inputs[0], gate_values[0], out_grad[0], filter_taps, skip_gain[None, :],
                *[jnp.asarray(table) for table in tables],
            )
        ],
    )
    input_part, gate_part, filter_part = pl.pallas_call(
        hand_over,
        out_shape=tuple(jax.ShapeDtypeStruct(part.shape, part.dtype) for part in results),
        in_specs=[near] * 3,
        out_specs=(anywhere,) * 3,
        scratch_shapes=[dma((3,))],
        compiler_params=pltpu.CompilerParams(vmem_limit_bytes=2 * 1024 * 1024),
    )(*results)
    return input_part[None], gate_part[None], filter_part.T


def solution(mesh):
    placed = (P("dp", "seq", None), P("dp", "seq", None), P("dp", "seq", None), P("seq", None), P())
    steps, replicas = mesh.shape["seq"], mesh.shape["dp"]

    def either(inputs, gate_values, out_grad, filter_taps, skip_gain):
        rows, width = filter_taps.shape
        fits = width == 128 and (steps, replicas) == (8, 4) and rows % 128 == 0
        if fits and inputs.shape[0] == 1:
            return fused(inputs, gate_values, out_grad, filter_taps, skip_gain, steps, replicas)
        return local(inputs, gate_values, out_grad, filter_taps, skip_gain)

    return jax.shard_map(
        either,
        mesh=mesh,
        in_specs=placed,
        out_specs=(P("dp", "seq", None), P("dp", "seq", None), P("seq", "dp")),
        check_vma=False,
    )
```

```python
import functools
import math

import jax
import jax.numpy as jnp
import ml_dtypes
import numpy as np
from jax import lax
from jax.experimental import pallas as pl
from jax.experimental.pallas import tpu as pltpu
from jax.sharding import PartitionSpec as P

first_radix = 32


def rotation(product, modulus, direction):
    fraction = (product % modulus).astype(jnp.float32) / modulus
    turned = 2.0 * math.pi * fraction
    return (jnp.cos(turned), direction * jnp.sin(turned))


def contract(formula, matrix, operand):
    return jnp.einsum(
        formula,
        matrix,
        operand,
        precision=lax.Precision.HIGHEST,
        preferred_element_type=jnp.float32,
    )


def complex_apply(formula, table_re, table_im, values_re, values_im):
    result_re = contract(formula, table_re, values_re) - contract(formula, table_im, values_im)
    result_im = contract(formula, table_re, values_im) + contract(formula, table_im, values_re)
    return (result_re, result_im)


def local_forward(values_re, values_im):
    pairs, rows, width = values_re.shape
    second = rows // first_radix
    values_re = values_re.reshape(pairs, first_radix, second, width)
    values_im = values_im.reshape(pairs, first_radix, second, width)
    outer = jnp.arange(first_radix, dtype=jnp.int32)
    inner = jnp.arange(second, dtype=jnp.int32)
    table_re, table_im = rotation(outer[:, None] * outer[None, :], first_radix, -1.0)
    section_re, section_im = complex_apply(
        "ca,mabx->mcbx", table_re, table_im, values_re, values_im
    )
    twist_re, twist_im = rotation(outer[:, None] * inner[None, :], rows, -1.0)
    twist_re = twist_re[None, :, :, None]
    twist_im = twist_im[None, :, :, None]
    turned_re = section_re * twist_re - section_im * twist_im
    turned_im = section_re * twist_im + section_im * twist_re
    table_re, table_im = rotation(inner[:, None] * inner[None, :], second, -1.0)
    return complex_apply("db,mcbx->mcdx", table_re, table_im, turned_re, turned_im)


def local_inverse(spec_re, spec_im):
    pairs, first, second, width = spec_re.shape
    rows = first * second
    outer = jnp.arange(first, dtype=jnp.int32)
    inner = jnp.arange(second, dtype=jnp.int32)
    table_re, table_im = rotation(inner[:, None] * inner[None, :], second, 1.0)
    section_re, section_im = complex_apply("bd,mcdx->mcbx", table_re, table_im, spec_re, spec_im)
    twist_re, twist_im = rotation(outer[:, None] * inner[None, :], rows, 1.0)
    twist_re = twist_re[None, :, :, None]
    twist_im = twist_im[None, :, :, None]
    turned_re = section_re * twist_re - section_im * twist_im
    turned_im = section_re * twist_im + section_im * twist_re
    table_re, table_im = rotation(outer[:, None] * outer[None, :], first, 1.0)
    result_re, result_im = complex_apply("ac,mcbx->mabx", table_re, table_im, turned_re, turned_im)
    return (result_re.reshape(pairs, rows, width), result_im.reshape(pairs, rows, width))


def frequency_labels():
    steps = lax.axis_size("seq")
    own = lax.axis_index("seq")
    local_labels = 2 * own + jnp.arange(2, dtype=jnp.int32)
    all_labels = jnp.arange(2 * steps, dtype=jnp.int32)
    return (local_labels, all_labels)


def forward_spectrum(signal):
    rows, width = signal.shape
    steps = lax.axis_size("seq")
    piece = rows // steps
    double = 2 * steps
    total = double * rows
    columns = lax.all_to_all(
        signal.reshape(1, rows, width), "seq", split_axis=1, concat_axis=0, tiled=True
    )
    block_index = jnp.arange(steps, dtype=jnp.int32)
    freq_index = jnp.arange(double, dtype=jnp.int32)
    table_re, table_im = rotation(freq_index[:, None] * block_index[None, :], double, -1.0)
    coarse_re = contract("kq,qrc->krc", table_re, columns)
    coarse_im = contract("kq,qrc->krc", table_im, columns)
    offsets = lax.axis_index("seq") * piece + jnp.arange(piece, dtype=jnp.int32)
    twist_re, twist_im = rotation(freq_index[:, None] * offsets[None, :], total, -1.0)
    twist_re = twist_re[:, :, None]
    twist_im = twist_im[:, :, None]
    turned_re = coarse_re * twist_re - coarse_im * twist_im
    turned_im = coarse_re * twist_im + coarse_im * twist_re
    moved = lax.all_to_all(
        jnp.stack([turned_re, turned_im]), "seq", split_axis=1, concat_axis=2, tiled=True
    )
    return local_forward(moved[0], moved[1])


def inverse_time(spec_re, spec_im, local_labels, all_labels):
    pairs, first, second, width = spec_re.shape
    rows = first * second
    steps = lax.axis_size("seq")
    double = 2 * steps
    total = double * rows
    time_re, time_im = local_inverse(spec_re, spec_im)
    positions = jnp.arange(rows, dtype=jnp.int32)
    twist_re, twist_im = rotation(local_labels[:, None] * positions[None, :], total, 1.0)
    twist_re = twist_re[:, :, None]
    twist_im = twist_im[:, :, None]
    turned_re = time_re * twist_re - time_im * twist_im
    turned_im = time_re * twist_im + time_im * twist_re
    moved = lax.all_to_all(
        jnp.stack([turned_re, turned_im]), "seq", split_axis=2, concat_axis=1, tiled=True
    )
    block_index = jnp.arange(steps, dtype=jnp.int32)
    table_re, table_im = rotation(block_index[:, None] * all_labels[None, :], double, 1.0)
    result_re = (
        contract("qk,krc->qrc", table_re, moved[0]) - contract("qk,krc->qrc", table_im, moved[1])
    ) / total
    result_im = (
        contract("qk,krc->qrc", table_re, moved[1]) + contract("qk,krc->qrc", table_im, moved[0])
    ) / total
    return (result_re, result_im)


def local(inputs, gate_values, out_grad, filter_taps, skip_gain):
    seq_input = inputs[0]
    seq_gate = gate_values[0]
    seq_grad = out_grad[0]
    rows, width = seq_input.shape
    replicas = lax.axis_size("dp")
    conv_grad = seq_grad * seq_gate
    spec_re, spec_im = forward_spectrum(
        jnp.concatenate([seq_input, conv_grad, filter_taps], axis=1)
    )
    filter_re = spec_re[..., 2 * width :]
    filter_im = spec_im[..., 2 * width :]
    input_re = spec_re[..., :width]
    input_im = spec_im[..., :width]
    grad_re = spec_re[..., width : 2 * width]
    grad_im = spec_im[..., width : 2 * width]
    conv_re = filter_re * input_re - filter_im * input_im
    conv_im = filter_re * input_im + filter_im * input_re
    corr_re = filter_re * grad_re + filter_im * grad_im
    corr_im = filter_re * grad_im - filter_im * grad_re
    taps_re = input_re * grad_re + input_im * grad_im
    taps_im = input_re * grad_im - input_im * grad_re
    packed_re = conv_re - corr_im
    packed_im = conv_im + corr_re
    local_labels, all_labels = frequency_labels()
    result_re, result_im = inverse_time(
        jnp.concatenate([packed_re, taps_re], axis=3),
        jnp.concatenate([packed_im, taps_im], axis=3),
        local_labels,
        all_labels,
    )
    results = jnp.concatenate([result_re, result_im[..., :width]], axis=2)
    timeline = lax.all_to_all(results, "seq", split_axis=0, concat_axis=1, tiled=True)[0]
    conv_time = timeline[:, :width]
    corr_time = timeline[:, timeline.shape[1] - width :]
    taps_time = timeline[:, width : timeline.shape[1] - width]
    taps_time = lax.psum_scatter(taps_time, "dp", scatter_dimension=1, tiled=True)
    gate_part = seq_grad * (conv_time + skip_gain[None, :] * seq_input)
    input_part = corr_time + skip_gain[None, :] * conv_grad
    length_total = rows * lax.axis_size("seq")
    batch_total = replicas * inputs.shape[0]
    filter_part = taps_time / math.sqrt(batch_total * length_total)
    return (input_part[None], gate_part[None], filter_part)


MESH = pl.DeviceIdType.MESH


def split_halves(table):
    high = table.astype(ml_dtypes.bfloat16)
    low = (table - high.astype(np.float64)).astype(ml_dtypes.bfloat16)
    return high, low


def block_tables(rows):
    double = 2 * rows
    place = np.arange(rows)
    turned = 2.0 * np.pi * ((place[:, None] * place[None, :]) % double) / double
    real = np.cos(turned)
    imag = -np.sin(turned)
    imag[:, 0] = 1.0 - 2.0 * (place % 2)
    forward = np.concatenate([real, imag], axis=1)
    weight = np.full((double, 1), 2.0 / double)
    weight[0] = weight[rows] = 1.0 / double
    inverse = forward.T * weight
    return split_halves(forward) + split_halves(inverse)


def dot3(values, high, low):
    top = values.astype(jnp.bfloat16)
    rest = (values - top.astype(jnp.float32)).astype(jnp.bfloat16)
    dot = functools.partial(jnp.dot, preferred_element_type=jnp.float32)
    both = dot(jnp.concatenate([top, rest], axis=0), high)
    count = values.shape[0]
    return both[:count] + (both[count:] + dot(top, low))


def kernel(
    steps, replicas, batch_total,
    in_any, gate_any, og_any, taps_any, skip_any, fh_any, fl_any, ih_any, il_any,
    ig_out, gg_out, fg_out,
    inp, gate, og, taps, skip, fh, fl, ih, il,
    sig, hsend, first_in, second_in, spec_first, spec_second, filt, prod, tprod,
    out_t, out_s, out_d, res, res_cross, res_taps, part,
    load_sem, h_send_sem, h_recv_sem, in_send_sem, in_recv_sem, out_send_sem, out_recv_sem,
    d_send_sem, d_recv_sem,
):
    devices = steps * replicas
    own_s = lax.axis_index("seq")
    own_d = lax.axis_index("dp")
    me = own_s * replicas + own_d
    rows, width = inp.shape
    lanes = 128
    half = steps // 2
    members = half * replicas
    side = own_s // half
    other = 1 - side
    place = me - members * side
    ahead = members // 2
    inner = jnp.where(side == 0, place >= ahead, place < ahead)
    cross_first = jnp.where(side == 0, 0, ahead)
    group = lax.rem(place + ahead, members)

    barrier = pltpu.get_barrier_semaphore()

    def greet(i, carry):
        p = lax.rem(me + i, devices)
        pl.semaphore_signal(
            barrier, inc=1, device_id=(p // replicas, lax.rem(p, replicas)), device_id_type=MESH
        )
        return carry

    loads = [
        pltpu.make_async_copy(src, dst, load_sem.at[k])
        for k, (src, dst) in enumerate([
            (taps_any, taps), (in_any, inp), (og_any, og), (gate_any, gate), (skip_any, skip),
            (fh_any, fh), (fl_any, fl), (ih_any, ih), (il_any, il),
        ])
    ]
    for copy in loads:
        copy.start()
    lax.fori_loop(1, devices, greet, 0, unroll=True)

    def remote(src, dst, src_sem, dst_sem, s, d):
        return pltpu.make_async_remote_copy(
            src_ref=src, dst_ref=dst, send_sem=src_sem, recv_sem=dst_sem,
            device_id=(s, d), device_id_type=MESH,
        )

    def arrived(ref, sem):
        pltpu.make_async_copy(ref, ref, sem).wait()

    def repeat(low, high, use, unroll=1):
        def body(i, carry):
            use(i)
            return carry

        lax.fori_loop(low, high, body, 0, unroll=unroll)

    def slot_of(block, of_side):
        return jnp.where(of_side == 0, steps - 1 - block, block)

    own_row = (slot_of(own_s, side) - half) * replicas + own_d
    cross_row = slot_of(own_s, other) * replicas + own_d
    h_row = lax.rem(own_s + half, steps)

    def group_at(s):
        return lax.rem(lax.rem(s, half) * replicas + own_d + ahead, members)

    h_low = jnp.where(side == 0, 0, half // 2)
    h_high = jnp.where(side == 0, steps, half + half // 2)

    def h_copy(s, sender):
        return remote(
            hsend.at[group_at(s)], first_in.at[h_row], h_send_sem.at[s], h_recv_sem.at[side], s, own_d
        )

    def h_each(use_remote, use_local):
        def body(s):
            @pl.when(s != own_s)
            def _():
                use_remote(s)

            if use_local is not None:
                @pl.when(s == own_s)
                def _():
                    use_local()

        repeat(h_low, h_high, body)

    def own_side(kind, which, dst_ref, base):
        def body(i):
            q = lax.rem(place + i, members)
            remote(
                sig.at[which, lax.rem(q + ahead, members)], dst_ref.at[base + own_row],
                in_send_sem.at[kind], in_recv_sem.at[kind],
                half * side + q // replicas, lax.rem(q, replicas),
            ).start()

        repeat(1, members, body, 5)
        pltpu.make_async_copy(sig.at[which, group], dst_ref.at[base + own_row], in_recv_sem.at[kind]).start()

    def crossing():
        def body(i):
            q = jnp.where(side == 0, 0, ahead) + lax.rem(lax.rem(place, ahead) + i, ahead)
            remote(
                sig.at[side, lax.rem(q + ahead, members)], second_in.at[cross_row],
                in_send_sem.at[2], in_recv_sem.at[2],
                half * other + q // replicas, lax.rem(q, replicas),
            ).start()

        repeat(0, ahead, body, 4)

    def prepare_input():
        loads[1].wait()
        sig[0] = inp[...].T.reshape(width // 8, 8, rows)

    def prepare_grad():
        loads[2].wait()
        loads[3].wait()
        gate[...] = og[...] * gate[...]
        sig[1] = gate[...].T.reshape(width // 8, 8, rows)

    loads[0].wait()
    hsend[...] = taps[...].T.reshape(width // 8, 8, rows)
    pl.when(side == 0)(prepare_input)
    pl.when(side == 1)(prepare_grad)
    pl.semaphore_wait(barrier, devices - 1)
    h_each(
        lambda s: h_copy(s, s).start(),
        lambda: pltpu.make_async_copy(hsend.at[group], first_in.at[h_row], h_recv_sem.at[side]).start(),
    )
    own_side(0, side, first_in, steps)
    crossing()
    pl.when(side == 0)(prepare_grad)
    pl.when(side == 1)(prepare_input)
    own_side(1, other, second_in, members)

    for copy in loads[4:]:
        copy.wait()

    lane = lax.broadcasted_iota(jnp.int32, (8, lanes), 1)
    sign = (1 - 2 * lax.rem(lane, 2)).astype(jnp.float32)
    turn = jnp.where(side == 0, 1.0, -1.0).astype(jnp.float32)

    def slices(c):
        re_at = pl.ds(pl.multiple_of(c * lanes, lanes), lanes)
        im_at = pl.ds(pl.multiple_of(rows + c * lanes, lanes), lanes)
        return re_at, im_at, (lane + c * lanes) == 0

    def add(total, term):
        return term if total is None else total + term

    def h_at(j):
        return (j + half) % steps

    def first_served(use):
        def body(i):
            q = lax.rem(place + i, members)
            pl.when(jnp.logical_and(q >= 6, q != place))(lambda: use(q))

        def served(q):
            pl.when(q != place)(lambda: use(q))

        repeat(0, 6, served)
        repeat(1, members, body, 5)

    def send_own(source, base, kind, which):
        def use(q):
            s = half * side + q // replicas
            at = (slot_of(s, side) - half) * replicas + lax.rem(q, replicas)
            remote(
                source.at[base + at], res.at[which, group], out_send_sem.at[kind], out_recv_sem.at[kind],
                s, lax.rem(q, replicas),
            ).start()

        first_served(use)
        pltpu.make_async_copy(source.at[base + own_row], res.at[which, group], out_recv_sem.at[kind]).start()

    def send_cross():
        def use(q):
            s = half * other + q // replicas
            at = slot_of(s, side) * replicas + lax.rem(q, replicas)
            remote(
                out_t.at[at], res_cross.at[lax.rem(place, ahead)], out_send_sem.at[2], out_recv_sem.at[2],
                s, lax.rem(q, replicas),
            ).start()

        repeat(0, 6, use)
        repeat(0, members, lambda i: pl.when(lax.rem(place + i, members) >= 6)(lambda: use(lax.rem(place + i, members))))

    d_dst = group // (members // replicas)
    d_at = lax.rem(group, members // replicas)

    def d_each(start, use_remote, use_local):
        def body(i):
            u = start + i
            to_self = jnp.logical_and(u == own_s, d_dst == own_d)

            @pl.when(jnp.logical_not(to_self))
            def _():
                use_remote(remote(
                    out_d.at[u], res_taps.at[d_at], d_send_sem.at[u], d_recv_sem.at[0], u, d_dst
                ))

            if use_local:
                @pl.when(to_self)
                def _():
                    pltpu.make_async_copy(out_d.at[u], res_taps.at[d_at], d_recv_sem.at[0]).start()

        repeat(0, half, body)

    def part_copy():
        return remote(
            out_d.at[pl.ds(0, half)], part, d_send_sem.at[0], d_recv_sem.at[1],
            lax.rem(own_s + half, steps), own_d,
        )

    def work(low):
        count = steps - low
        def transform_first(start, size):
            spec_first[pl.ds(start, size)] = dot3(
                first_in[pl.ds(start, size)].reshape(size * 8, rows), fh[...], fl[...]
            ).reshape(size, 8, 2 * rows)

        arrived(first_in.at[pl.ds(half, half)], h_recv_sem.at[0])
        if low == 0:
            arrived(first_in.at[pl.ds(0, half)], h_recv_sem.at[1])
        transform_first(low, count)

        def prepare(c):
            re_at, im_at, first = slices(c)
            re = [spec_first[h_at(j), :, re_at] for j in range(count)]
            im = [spec_first[h_at(j), :, im_at] for j in range(count)]
            for j in range(count):
                out_re = re[j] if j == 0 else re[j] + sign * re[j - 1]
                out_im = im[j] if j == 0 else im[j] + sign * im[j - 1]
                filt[0, j, :, re_at] = out_re
                filt[1, j, :, re_at] = jnp.where(first, 0.0, turn * out_im)
                filt[2, j, :, re_at] = jnp.where(first, out_im, out_re)

        repeat(0, rows // lanes, prepare)
        arrived(first_in.at[pl.ds(steps, members)], in_recv_sem.at[0])
        transform_first(steps, members)

        def filters(re_at):
            return [[filt[i, j, :, re_at] for j in range(count)] for i in range(3)]

        def first_products(i):
            c, k = i // replicas, lax.rem(i, replicas)
            re_at, im_at, _ = slices(c)
            h_re, h_im, h_re2 = filters(re_at)
            t_re = [spec_first[steps + v * replicas + k, :, re_at] for v in range(half)]
            t_im = [spec_first[steps + v * replicas + k, :, im_at] for v in range(half)]
            for u in range(low, steps):
                re, im = None, None
                for v in range(max(u, half), steps):
                    j, w = v - u, v - half
                    re = add(re, h_re[j] * t_re[w] - h_im[j] * t_im[w])
                    im = add(im, h_re2[j] * t_im[w] + h_im[j] * t_re[w])
                prod[u * replicas + k, :, re_at] = re
                prod[u * replicas + k, :, im_at] = im

        repeat(0, rows // lanes * replicas, first_products, 4)

        def inverse(source, start, size):
            return dot3(
                source[pl.ds(start, size)].reshape(size * 8, 2 * rows), ih[...], il[...]
            ).reshape(size, 8, rows)

        if low == 0:
            out_t[...] = inverse(prod, 0, 2 * members)
            send_cross()
        else:
            out_t[pl.ds(members, members)] = inverse(prod, members, members)
        send_own(out_t, members, 0, side)

        def transform(start):
            spec_second[pl.ds(start, members)] = dot3(
                second_in[pl.ds(start, members)].reshape(members * 8, rows), fh[...], fl[...]
            ).reshape(members, 8, 2 * rows)

        def second_products(begin, end, extend):
            def body(i):
                c, k = i // replicas, lax.rem(i, replicas)
                re_at, im_at, _ = slices(c)
                h_re, h_im, h_re2 = filters(re_at)
                s_re = [spec_second[v * replicas + k, :, re_at] for v in range(begin, end)]
                s_im = [spec_second[v * replicas + k, :, im_at] for v in range(begin, end)]
                for u in range(half, steps):
                    at = (u - half) * replicas + k
                    re, im = (prod[at, :, re_at], prod[at, :, im_at]) if extend else (None, None)
                    for v in range(begin, min(u + 1, end)):
                        j, w = u - v, v - begin
                        re = add(re, h_re[j] * s_re[w] + h_im[j] * s_im[w])
                        im = add(im, h_re2[j] * s_im[w] - h_im[j] * s_re[w])
                    prod[at, :, re_at] = re
                    prod[at, :, im_at] = im

            repeat(0, rows // lanes * replicas, body, 4)

        def taps_products(begin, end, extend):
            def body(c):
                re_at, im_at, first = slices(c)
                flip = jnp.where(first, 1.0, -turn)
                sums_re, sums_im = [None] * (steps + 1), [None] * (steps + 1)
                for k in range(replicas):
                    t_re = [spec_first[steps + v * replicas + k, :, re_at] for v in range(half)]
                    t_im = [spec_first[steps + v * replicas + k, :, im_at] for v in range(half)]
                    for s in range(begin, end):
                        s_re = spec_second[s * replicas + k, :, re_at]
                        s_im = spec_second[s * replicas + k, :, im_at]
                        s_re2 = jnp.where(first, s_im, s_re)
                        s_im = jnp.where(first, 0.0, s_im)
                        for v in range(max(s, half), steps):
                            m, w = v - s, v - half
                            sums_re[m] = add(sums_re[m], t_re[w] * s_re + t_im[w] * s_im)
                            sums_im[m] = add(sums_im[m], t_im[w] * s_re2 - t_re[w] * s_im)

                def folded(sums, m):
                    if sums[m] is None:
                        return sign * sums[m + 1]
                    return sums[m] if sums[m + 1] is None else sums[m] + sign * sums[m + 1]

                for m in range(half if end == steps else steps):
                    re, im = folded(sums_re, m), flip * folded(sums_im, m)
                    tprod[m, :, re_at] = tprod[m, :, re_at] + re if extend else re
                    tprod[m, :, im_at] = tprod[m, :, im_at] + im if extend else im

            repeat(0, rows // lanes, body)

        def finish_second():
            second_products(half, steps, low == 0)
            out_s[...] = inverse(prod, 0, members)
            send_own(out_s, 0, 1, other)

        def finish_taps():
            taps_products(half, steps, low == 0)
            out_d[pl.ds(0, half)] = inverse(tprod, 0, half)
            if low == 0:
                arrived(part, d_recv_sem.at[1])
                out_d[pl.ds(0, half)] = out_d[pl.ds(0, half)] + part[...]
                d_each(0, lambda copy: copy.start(), True)
            else:
                part_copy().start()

        if low == 0:
            arrived(second_in.at[pl.ds(0, members)], in_recv_sem.at[2])
            transform(0)
            taps_products(0, half, False)
            out_d[pl.ds(half, half)] = inverse(tprod, half, half)
            d_each(half, lambda copy: copy.start(), True)
            second_products(0, half, False)
        arrived(second_in.at[pl.ds(members, members)], in_recv_sem.at[1])
        transform(members)
        if low == 0:
            finish_taps()
            finish_second()
        else:
            finish_taps()
            finish_second()

    pl.when(inner)(lambda: work(0))
    pl.when(jnp.logical_not(inner))(lambda: work(half))

    gain = skip[...]

    def positions(which):
        return res[which].reshape(width, rows).T

    def finish(is_second):
        ranges = pl.ds(0, ahead) if is_second else pl.ds(ahead, ahead)
        arrived(res.at[1 if is_second else 0], out_recv_sem.at[0])
        if is_second:
            ig_out[...] = positions(1) + gain * gate[...]
        else:
            gg_out[...] = og[...] * (positions(0) + gain * inp[...])
        late = 0 if is_second else 1
        scale = 1.0 / math.sqrt(batch_total * rows * steps)
        arrived(res_taps, d_recv_sem.at[0])
        fg_out[...] = scale * res_taps[...].reshape(width // replicas, rows)
        arrived(res_cross, out_recv_sem.at[2])
        arrived(res.at[late], out_recv_sem.at[1])
        res[late, ranges] = res[late, ranges] + res_cross[...]
        if is_second:
            gg_out[...] = og[...] * (positions(0) + gain * inp[...])
        else:
            ig_out[...] = positions(1) + gain * gate[...]

    h_each(lambda s: h_copy(s, s).wait_send(), None)
    arrived(sig.at[0, pl.ds(0, members - 1)], in_send_sem.at[0])
    arrived(sig.at[0, pl.ds(0, members - 1)], in_send_sem.at[1])
    arrived(sig.at[0, pl.ds(0, ahead)], in_send_sem.at[2])

    @pl.when(inner)
    def _():
        d_each(half, lambda copy: copy.wait_send(), False)

    pl.when(side == 0)(lambda: finish(False))
    pl.when(side == 1)(lambda: finish(True))

    arrived(sig.at[0, pl.ds(0, members - 1)], out_send_sem.at[0])
    arrived(sig.at[0, pl.ds(0, members - 1)], out_send_sem.at[1])

    @pl.when(inner)
    def _():
        arrived(sig.at[0], out_send_sem.at[2])
        d_each(0, lambda copy: copy.wait_send(), False)

    @pl.when(jnp.logical_not(inner))
    def _():
        part_copy().wait_send()


def hand_over(*refs):
    writes = [pltpu.make_async_copy(refs[k], refs[3 + k], refs[6].at[k]) for k in range(3)]
    for copy in writes:
        copy.start()
    for copy in writes:
        copy.wait()


def fused(inputs, gate_values, out_grad, filter_taps, skip_gain, steps, replicas):
    rows, width = filter_taps.shape
    double = 2 * rows
    members = steps * replicas // 2
    tables = block_tables(rows)
    f32, bf16 = jnp.float32, jnp.bfloat16
    dma = pltpu.SemaphoreType.DMA
    anywhere = pl.BlockSpec(memory_space=pltpu.HBM)
    near = pl.BlockSpec(memory_space=pltpu.VMEM)
    block = pltpu.VMEM((rows, width), f32)

    def tiles(*shape):
        return pltpu.VMEM(shape + (8, rows), f32)

    def spectra(count):
        return pltpu.VMEM((count, 8, double), f32)

    results = pl.pallas_call(
        functools.partial(kernel, steps, replicas, replicas * inputs.shape[0]),
        out_shape=(
            pltpu.VMEM((rows, width), f32),
            pltpu.VMEM((rows, width), f32),
            pltpu.VMEM((width // replicas, rows), f32),
        ),
        in_specs=[anywhere] * 9,
        out_specs=(near, near, near),
        scratch_shapes=[block, block, block, block, pltpu.VMEM((1, width), f32)]
        + [pltpu.VMEM((rows, double), bf16)] * 2
        + [pltpu.VMEM((double, rows), bf16)] * 2
        + [tiles(2, width // 8), tiles(width // 8), tiles(steps + members), tiles(2 * members)]
        + [spectra(steps + members), spectra(2 * members), tiles(3, steps)]
        + [spectra(2 * members), spectra(steps)]
        + [tiles(2 * members), tiles(members), tiles(steps)]
        + [tiles(2, width // 8), tiles(width // 16), tiles(width // 8 // replicas), tiles(steps // 2)]
        + [dma((9,)), dma((steps,)), dma((2,)), dma((3,)), dma((3,)), dma((3,)), dma((3,)), dma((steps,)), dma((2,))],
        compiler_params=pltpu.CompilerParams(
            collective_id=0, has_side_effects=True, vmem_limit_bytes=48 * 1024 * 1024
        ),
    )(
        *[
            pltpu.with_memory_space_constraint(value, pltpu.HBM)
            for value in (
                inputs[0], gate_values[0], out_grad[0], filter_taps, skip_gain[None, :],
                *[jnp.asarray(table) for table in tables],
            )
        ],
    )
    input_part, gate_part, filter_part = pl.pallas_call(
        hand_over,
        out_shape=tuple(jax.ShapeDtypeStruct(part.shape, part.dtype) for part in results),
        in_specs=[near] * 3,
        out_specs=(anywhere,) * 3,
        scratch_shapes=[dma((3,))],
        compiler_params=pltpu.CompilerParams(vmem_limit_bytes=2 * 1024 * 1024),
    )(*results)
    return input_part[None], gate_part[None], filter_part.T


def solution(mesh):
    placed = (P("dp", "seq", None), P("dp", "seq", None), P("dp", "seq", None), P("seq", None), P())
    steps, replicas = mesh.shape["seq"], mesh.shape["dp"]

    def either(inputs, gate_values, out_grad, filter_taps, skip_gain):
        rows, width = filter_taps.shape
        fits = width == 128 and (steps, replicas) == (8, 4) and rows % 128 == 0
        if fits and inputs.shape[0] == 1:
            return fused(inputs, gate_values, out_grad, filter_taps, skip_gain, steps, replicas)
        return local(inputs, gate_values, out_grad, filter_taps, skip_gain)

    return jax.shard_map(
        either,
        mesh=mesh,
        in_specs=placed,
        out_specs=(P("dp", "seq", None), P("dp", "seq", None), P("seq", "dp")),
        check_vma=False,
    )
```
